512 devices in a mesh: grp: 16 (over y, core), wide: 32 (over z, x).
Axes of the slice: x: 4, y: 8, z: 8, core: 2. Of those that a mesh axis runs over, the one named last changes fastest.
Arguments:
- three_center: float32 [64, 1280, 256], P(None, 'wide'), may hold values from -0.6 to 0.6
- counts: int32 [32], replicated, may hold values from 1 to 40, 1024 in all
- occ_energy: float32 [64], replicated, may hold values from -2 to -0.5
- virt_energy: float32 [256], replicated, may hold values from 0.5 to 3
- match_tables: int32 [2, 16, 32], P(None, 'grp'), may hold values from 0 to 31, as said below
Outputs:
- gradient: float32 [64, 1024, 256], P('wide', 'grp')
The draws below stay inside these ranges and needn't reach their ends.
Inputs may be any that keep to these rules, and one draw needn't show every extreme that they name: counts sum to 1024; the largest is 40. Each row match_tables[k, g, :] is a perfect matching of the 32 blocks: no block is its own partner, and the partner of the partner is the block itself.
All inputs are finite; a program needn't handle non-finite values.
Results may differ from the reference program's by a relative error of at most 0.0003.
Values sent between devices are 32-bit elements; how exact they have to be, the bound alone decides.
No kernel may reach another device: no remote copies, remote signals or barrier semaphores. Data moves between devices by JAX's collectives and lax.ppermute only.
A program may use at most 64 MiB of HBM per device.

```python
import math
import jax
import jax.numpy as jnp
import numpy as np
from jax import lax

NAUX = 1024
V = 256
OCC_DEV = 2
MATCH = 2
O = 64
CAP = 40
N_GRP = 16
N_WIDE = 32


def draw_match_tables(key, part):
    keys = jax.random.split(jax.random.fold_in(key, 17), MATCH * N_GRP)

    def one_matching(one_key):
        order = jax.random.permutation(one_key, N_WIDE).astype(jnp.int32)
        firsts = order[0::2]
        seconds = order[1::2]
        partner = jnp.zeros((N_WIDE,), jnp.int32)
        partner = partner.at[firsts].set(seconds)
        partner = partner.at[seconds].set(firsts)
        return partner
    return jax.vmap(one_matching)(keys).reshape(MATCH, N_GRP, N_WIDE)


def shard_levels(stream_key, shape, cuts, smallest, high):
    level = 1.0
    for axis_at, blocks in cuts:
        steps = jax.random.uniform(jax.random.fold_in(jax.random.fold_in(stream_key, 6), axis_at), (blocks,), jnp.float32, smallest / len(cuts), high / len(cuts))
        level = level * jnp.repeat(jnp.exp(steps), shape[axis_at] // blocks).reshape((-1,) + (1,) * (len(shape) - 1 - axis_at))
    return level


def split_up(number_of, total, most, slope):
    portions = [(1 << 20) // math.isqrt(standing ** slope) + 1 for standing in range(2, number_of + 1)]
    surplus, given = total - most - (number_of - 1), [1] * (number_of - 1)
    while surplus > 0:
        movable = [i for i in range(number_of - 1) if given[i] < most]
        pool, remaining = sum([portions[i] for i in movable]), surplus
        for i in movable:
            extra = min(most - given[i], max(1, remaining * portions[i] // pool), surplus)
            given[i] = given[i] + extra
            surplus = surplus - extra
    return np.array([most] + given)


def ragged_sizes(own_key, count, total, limit, slope):
    if count == 2:
        one = jax.random.randint(own_key, (), max(1, total - limit), min(limit, total - 1) + 1)
        return jnp.stack([one, total - one])
    lengths = jnp.asarray(split_up(count, total, limit, slope), jnp.int32)
    pairs = (count - 1) // 2
    source_of, taker = lengths[1:1 + 2 * pairs:2], lengths[2:2 + 2 * pairs:2]
    room = jnp.minimum(source_of - 1, limit - taker)
    shifted = jax.random.randint(jax.random.fold_in(own_key, 1), (pairs,), 0, 1 << 20) % (room + 1)
    lengths = lengths.at[1:1 + 2 * pairs:2].set(source_of - shifted).at[2:2 + 2 * pairs:2].set(taker + shifted)
    return lengths[jax.random.permutation(jax.random.fold_in(own_key, 2), count)]


def bell_draw(own_key, dims, width, bound, shards=(), kind=jnp.bfloat16):
    values = jax.random.normal(own_key, dims, jnp.float32) * width
    if len(shards) > 0:
        values = shard_levels(own_key, dims, shards, -0.22, 0.18) * values
    return jnp.clip(values, min=-bound, max=bound).astype(kind)


def setup_inputs(seed: int = 0) -> dict:
    key_of = jax.random.split(jax.random.key(seed), 6)
    three_center = bell_draw(key_of[0], (O, N_WIDE * CAP, V), 0.1, 0.6, ((1, 32),), jnp.float32)
    counts = ragged_sizes(key_of[1], N_WIDE, NAUX, CAP, 2).astype(jnp.int32)
    occ_energy = jnp.clip(jax.random.uniform(key_of[2], (O,), jnp.float32, -2.0, -0.5), -2.0, -0.5)
    virt_energy = jnp.clip(jax.random.uniform(key_of[3], (V,), jnp.float32, 0.5, 3.0), 0.5, 3.0)
    match_tables = draw_match_tables(jax.random.fold_in(key_of[5], 71), 0)
    return dict(three_center=three_center, counts=counts, occ_energy=occ_energy, virt_energy=virt_energy, match_tables=match_tables)


def pair_term(own_block, partner_block, own_energy, partner_energy, virt_energy):
    highest = lax.Precision.HIGHEST
    coulomb = jnp.einsum('ipa,jpb->ijab', own_block, partner_block, precision=highest, preferred_element_type=jnp.float32)
    denom = (own_energy[:, None, None, None] + partner_energy[None, :, None, None]
             - virt_energy[None, None, :, None] - virt_energy[None, None, None, :])
    amplitude = coulomb / denom
    combined = 2.0 * amplitude - jnp.swapaxes(amplitude, 2, 3)
    return jnp.einsum('ijab,jpb->ipa', combined, partner_block, precision=highest, preferred_element_type=jnp.float32)


def compact_rows(padded, counts):
    counts = counts.astype(jnp.int32)
    offsets = (jnp.cumsum(counts) - counts).astype(jnp.int32)
    aux_rows = jnp.arange(NAUX, dtype=jnp.int32)
    source = (jnp.sum((offsets[None, :] <= aux_rows[:, None]).astype(jnp.int32), axis=1) - 1).astype(jnp.int32)
    slots = jnp.arange(N_WIDE, dtype=jnp.int32)
    starts = jnp.sum(jnp.where(slots[None, :] == source[:, None], offsets[None, :], 0), axis=1).astype(jnp.int32)
    gather_index = (source * CAP + aux_rows - starts).astype(jnp.int32)
    return jnp.take(padded, gather_index, axis=1)


def reference(three_center, counts, occ_energy, virt_energy, match_tables):
    dense = compact_rows(three_center, counts)
    blocks = dense.reshape(N_WIDE, OCC_DEV, NAUX, V)
    energies = occ_energy.reshape(N_WIDE, OCC_DEV)
    partner_lists = match_tables.reshape(MATCH * N_GRP, N_WIDE)

    def per_block(block_id):
        own_block = blocks[block_id]
        own_energy = energies[block_id]
        total = pair_term(own_block, own_block, own_energy, own_energy, virt_energy)

        def per_pair(accum, partner_id):
            return accum + pair_term(own_block, blocks[partner_id], own_energy, energies[partner_id], virt_energy), None

        total, _ = lax.scan(per_pair, total, partner_lists[:, block_id].astype(jnp.int32))
        return total

    result = lax.map(per_block, jnp.arange(N_WIDE, dtype=jnp.int32))
    return result.reshape(O, NAUX, V)
```

```python
import jax
import jax.numpy as jnp
import numpy as np
from jax import lax
from jax.experimental import pallas as pl
from jax.experimental.pallas import tpu as pltpu
from jax.sharding import Mesh, PartitionSpec as P

NAUX = 1024
OCC_DEV = 2
CAP = 40
V = 256
NY, NC, NZ, NX = 8, 2, 8, 4
BLK = 64
PAD = 48
MIB = 1 << 20


def split_hi_lo(x):
    hi = x.astype(jnp.bfloat16)
    lo = (x - hi.astype(jnp.float32)).astype(jnp.bfloat16)
    return hi, lo


def dot3(ah, al, bh, bl):
    def mm(a, b):
        return lax.dot_general(a, b, (((1,), (0,)), ((), ())), preferred_element_type=jnp.float32)

    return mm(ah, bh) + mm(ah, bl) + mm(al, bh)


def put_rows(dense, off, cols, block):
    base = pl.multiple_of(off // 8 * 8, 8)
    shift = off - base
    before = lax.broadcasted_iota(jnp.int32, (8, block.shape[1]), 0) < shift
    held = dense[pl.ds(base, 8), cols]
    for k in range(CAP // 8):
        turned = pltpu.roll(block[k * 8:(k + 1) * 8, :], shift, 0)
        dense[pl.ds(base + k * 8, 8), cols] = jnp.where(before, held, turned)
        held = turned
    dense[pl.ds(base + CAP, 8), cols] = held


def own_rows_kernel(place, counts, own_ref, other_ref, hi_ref, lo_ref, dense):
    core, u = place[0], place[1]

    def put(s, off):
        g = lax.rem(s + u, 16)
        t = lax.rem(s // 16 + u // 16, 2)
        y = g // 2

        def copy(ref):
            for i in range(OCC_DEV):
                rows = ref[y, pl.ds(pl.multiple_of((t * OCC_DEV + i) * CAP, 8), CAP), :]
                put_rows(dense, off, slice(i * V, (i + 1) * V), rows)

        @pl.when(lax.rem(g, 2) == core)
        def _():
            copy(own_ref)

        @pl.when(lax.rem(g, 2) != core)
        def _():
            copy(other_ref)

        return off + counts[s]

    lax.fori_loop(0, 32, put, jnp.int32(0))

    def turn(n, carry):
        k, pair = n // 4, n % 4
        first = pl.multiple_of((4 * pair + lax.rem(core + 1 + k, 2)) * BLK, BLK)
        rows = jnp.concatenate(
            [dense[pl.ds(first, BLK), :], dense[pl.ds(first + 2 * BLK, BLK), :]], axis=0
        )
        hi, lo = split_hi_lo(rows.T)
        hi_ref[:, n * 128:(n + 1) * 128] = hi
        lo_ref[:, n * 128:(n + 1) * 128] = lo
        return carry

    for n in range(8):
        turn(n, 0)


def pair_kernel(place, counts, occ, own_hi, own_lo, own_pay, other_pay, virt, wide_ref,
                theirs_ref, mine_ref, dense, w_hi, w_lo, x_hi, x_lo):
    core, u, grp = place[0], place[1], place[2]

    def put(s, off):
        for j in range(4):
            put_rows(dense, off, slice(j * V, (j + 1) * V), wide_ref[s, j])
        return off + counts[s]

    lax.fori_loop(0, 32, put, jnp.int32(0))

    def split(n, carry):
        k, y = n // 8, lax.rem(n, 8)
        src = pl.multiple_of((2 * y + lax.rem(core + 1 + k, 2)) * BLK, BLK)
        dst = pl.multiple_of(n * BLK, BLK)
        hi, lo = split_hi_lo(dense[pl.ds(src, BLK), :])
        w_hi[pl.ds(dst, BLK), :] = hi
        w_lo[pl.ds(dst, BLK), :] = lo
        return carry

    lax.fori_loop(0, 16, split, 0)

    virt_row = jnp.broadcast_to(virt[...], (V, V))
    virt_sum = virt_row + virt_row.T
    for w in range(2):
        block = (2 * grp + w).astype(jnp.float32)
        hits = jnp.zeros((8, V), jnp.float32)
        for y in range(NY):
            for pay in (own_pay, other_pay):
                hits = hits + (pay[y, 4 * CAP:4 * CAP + 8, :] == block).astype(jnp.float32)
        times = hits[:1, :128] + hits[:1, 128:] + (u == 2 * grp + w).astype(jnp.float32)
        times = jnp.concatenate([times, times], axis=1)
        for jj in range(2):
            j = 2 * w + jj
            cols = slice(j * V, (j + 1) * V)
            coulomb = dot3(own_hi[...], own_lo[...], w_hi[:, cols], w_lo[:, cols])
            for i in range(OCC_DEV):
                c = coulomb[i * V:(i + 1) * V, :]
                scale = times / ((occ[2 * u + i] + occ[4 * grp + j]) - virt_sum)
                hi, lo = split_hi_lo((2.0 * c.T - c) * scale)
                x_hi[cols, i * V:(i + 1) * V] = hi
                x_lo[cols, i * V:(i + 1) * V] = lo

    for k, out in enumerate((theirs_ref, mine_ref)):
        for half in range(2):
            rows = slice(k * 512 + half * 256, k * 512 + half * 256 + 256)
            term = dot3(w_hi[rows, :], w_lo[rows, :], x_hi[...], x_lo[...])
            for q in range(4):
                for i in range(OCC_DEV):
                    out[half * 4 + q, i] = term[q * BLK:(q + 1) * BLK, i * V:(i + 1) * V]


def per_device(three_center, counts, occ_energy, virt_energy, match_tables):
    y, c = lax.axis_index("y"), lax.axis_index("c")
    z, x = lax.axis_index("z"), lax.axis_index("x")
    grp, pos = y * NC + c, z * NX + x
    place = jnp.stack([c, pos, grp]).astype(jnp.int32)

    wide_part = lax.dynamic_slice_in_dim(three_center, 4 * grp, 4, 0)
    wide_all = lax.all_gather(wide_part, ("z", "x"))

    axes = ("y", "c", "z", "x")
    got = []
    for t in range(2):
        to = lax.rem(grp - pos + 32, 16) + 16 * lax.rem(pos // 16 + t, 2)
        piece = lax.dynamic_slice_in_dim(three_center, OCC_DEV * to, OCC_DEV, 0)
        perm = [
            (g * 32 + s, g * 32 + (g - s) % 16 + 16 * ((s // 16 + t) % 2))
            for g in range(16) for s in range(32)
        ]
        got.append(lax.ppermute(piece, axes, perm).reshape(OCC_DEV * CAP, V))
    partners = lax.dynamic_slice_in_dim(match_tables[:, 0, :], pos, 1, 1).astype(jnp.float32)
    note = jnp.broadcast_to(jnp.repeat(partners.reshape(1, 2), 128, axis=1), (8, V))
    load = jnp.concatenate(got + [note], axis=0)
    sent = jnp.broadcast_to(load[None], (NY, 4 * CAP + 8, V))
    own_pay = lax.all_to_all(sent, "y", split_axis=0, concat_axis=0, tiled=True)
    other_pay = lax.ppermute(own_pay, "c", [(0, 1), (1, 0)])

    smem = pl.BlockSpec(memory_space=pltpu.SMEM)
    vmem = pl.BlockSpec(memory_space=pltpu.VMEM)
    own_hi, own_lo = pl.pallas_call(
        own_rows_kernel,
        out_shape=[jax.ShapeDtypeStruct((OCC_DEV * V, NAUX), jnp.bfloat16)] * 2,
        in_specs=[smem, smem, vmem, vmem],
        out_specs=[vmem, vmem],
        scratch_shapes=[pltpu.VMEM((NAUX + PAD, OCC_DEV * V), jnp.float32)],
        compiler_params=pltpu.CompilerParams(vmem_limit_bytes=24 * MIB),
        name="own_rows",
    )(place, counts, own_pay, other_pay)

    part = jax.ShapeDtypeStruct((NY, OCC_DEV, BLK, V), jnp.float32)
    theirs, mine = pl.pallas_call(
        pair_kernel,
        out_shape=[part, part],
        in_specs=[smem] * 3 + [vmem] * 6,
        out_specs=[vmem, vmem],
        scratch_shapes=[
            pltpu.VMEM((NAUX + PAD, 4 * V), jnp.float32),
            pltpu.VMEM((NAUX, 4 * V), jnp.bfloat16),
            pltpu.VMEM((NAUX, 4 * V), jnp.bfloat16),
            pltpu.VMEM((4 * V, OCC_DEV * V), jnp.bfloat16),
            pltpu.VMEM((4 * V, OCC_DEV * V), jnp.bfloat16),
        ],
        compiler_params=pltpu.CompilerParams(vmem_limit_bytes=48 * MIB),
        name="pairs",
    )(place, counts, occ_energy, own_hi, own_lo, own_pay, other_pay,
      virt_energy.reshape(1, V), wide_all)

    mine = mine + lax.ppermute(theirs, "c", [(0, 1), (1, 0)])
    pieces = lax.all_to_all(mine, "y", split_axis=0, concat_axis=0, tiled=True)
    return jnp.sum(pieces, axis=0)


def solution(mesh):
    fine = Mesh(np.asarray(mesh.devices).reshape(NY, NC, NZ, NX), ("y", "c", "z", "x"))
    wide, grp = ("z", "x"), ("y", "c")
    placed = (P(None, wide, None), P(), P(), P(), P(None, grp, None))
    return jax.shard_map(
        per_device, mesh=fine, in_specs=placed, out_specs=P(wide, grp, None), check_vma=False
    )
```

```python
import functools

import jax
import jax.numpy as jnp
import numpy as np
from jax import lax
from jax.experimental import pallas as pl
from jax.experimental.pallas import tpu as pltpu
from jax.sharding import Mesh, PartitionSpec as P

NAUX = 1024
OCC_DEV = 2
CAP = 40
V = 256
NY, NC, NZ, NX = 8, 2, 8, 4
BLK = 64
PAD = 48
MIB = 1 << 20


def split_hi_lo(x):
    hi = x.astype(jnp.bfloat16)
    lo = (x - hi.astype(jnp.float32)).astype(jnp.bfloat16)
    return hi, lo


def dot3(ah, al, bh, bl):
    def mm(a, b):
        return lax.dot_general(a, b, (((1,), (0,)), ((), ())), preferred_element_type=jnp.float32)

    return mm(ah, bh) + mm(ah, bl) + mm(al, bh)


def put_rows(dense, off, cols, block):
    base = pl.multiple_of(off // 8 * 8, 8)
    shift = off - base
    before = lax.broadcasted_iota(jnp.int32, (8, block.shape[1]), 0) < shift
    held = dense[pl.ds(base, 8), cols]
    for k in range(CAP // 8):
        turned = pltpu.roll(block[k * 8:(k + 1) * 8, :], shift, 0)
        dense[pl.ds(base + k * 8, 8), cols] = jnp.where(before, held, turned)
        held = turned
    dense[pl.ds(base + CAP, 8), cols] = held


def own_rows_kernel(place, counts, own_ref, other_ref, hi_out, lo_out, dense, hi_ref, lo_ref, sems):
    core, u = place[0], place[1]

    def put(s, off):
        g = lax.rem(s + u, 16)
        t = lax.rem(s // 16 + u // 16, 2)
        y = g // 2

        def copy(ref):
            for i in range(OCC_DEV):
                rows = ref[y, pl.ds(pl.multiple_of((t * OCC_DEV + i) * CAP, 8), CAP), :]
                put_rows(dense, off, slice(i * V, (i + 1) * V), rows)

        @pl.when(lax.rem(g, 2) == core)
        def _():
            copy(own_ref)

        @pl.when(lax.rem(g, 2) != core)
        def _():
            copy(other_ref)

        return off + counts[s]

    lax.fori_loop(0, 32, put, jnp.int32(0))

    def turn(n, carry):
        k, pair = n // 4, n % 4
        first = pl.multiple_of((4 * pair + lax.rem(core + 1 + k, 2)) * BLK, BLK)
        rows = jnp.concatenate(
            [dense[pl.ds(first, BLK), :], dense[pl.ds(first + 2 * BLK, BLK), :]], axis=0
        )
        hi, lo = split_hi_lo(rows.T)
        hi_ref[:, n * 128:(n + 1) * 128] = hi
        lo_ref[:, n * 128:(n + 1) * 128] = lo
        return carry

    for n in range(8):
        turn(n, 0)
    copies = [
        pltpu.make_async_copy(hi_ref, hi_out, sems.at[0]),
        pltpu.make_async_copy(lo_ref, lo_out, sems.at[1]),
    ]
    for copy in copies:
        copy.start()
    for copy in copies:
        copy.wait()


def block_kernel(first, place, counts, occ, own_hi_any, own_lo_any, own_pay, other_pay, virt, *refs):
    n_wide = 1 if first else 9
    wide, refs = refs[:n_wide], refs[n_wide:]
    before, refs = ((), refs) if first else (refs[:2], refs[2:])
    outs, (own_hi, own_lo, rows, dense, w_hi, w_lo, x_hi, x_lo, sems) = refs[:2], refs[2:]
    core, u, grp, z_here = place[0], place[1], place[2], place[3]

    own_copies = [
        pltpu.make_async_copy(own_hi_any, own_hi, sems.at[0]),
        pltpu.make_async_copy(own_lo_any, own_lo, sems.at[1]),
    ]
    if first:
        row_copies = [
            pltpu.make_async_copy(wide[0].at[k], rows.at[k], sems.at[2 + k]) for k in range(NZ)
        ]
    else:
        steps = (0, -1, -2, -3, 1, 2, 3)
        row_copies = [
            pltpu.make_async_copy(wide[k], rows.at[lax.rem(z_here + d + NZ, NZ)], sems.at[2 + k])
            for k, d in enumerate(steps)
        ]
        z_far = lax.rem(z_here + 4, NZ)
        row_copies += [
            pltpu.make_async_copy(wide[7 + i], rows.at[z_far, :, pl.ds(i, 1)], sems.at[9 + i])
            for i in range(2)
        ]
    for copy in row_copies + own_copies:
        copy.start()
    if not first:
        for copy in row_copies:
            copy.wait()

    off = jnp.int32(0)
    for z in range(NZ):
        if first:
            row_copies[z].wait()

        def put(k, off):
            for j in range(OCC_DEV):
                put_rows(dense, off, slice(j * V, (j + 1) * V), rows[z, k, j])
            return off + counts[z * NX + k]

        off = lax.fori_loop(0, NX, put, off)

    def split(n, carry):
        k, y = n // 8, lax.rem(n, 8)
        src = pl.multiple_of((2 * y + lax.rem(core + 1 + k, 2)) * BLK, BLK)
        dst = pl.multiple_of(n * BLK, BLK)
        hi, lo = split_hi_lo(dense[pl.ds(src, BLK), :])
        w_hi[pl.ds(dst, BLK), :] = hi
        w_lo[pl.ds(dst, BLK), :] = lo
        return carry

    lax.fori_loop(0, 16, split, 0)

    virt_row = jnp.broadcast_to(virt[...], (V, V))
    virt_sum = virt_row + virt_row.T
    w = 2 * grp + (0 if first else 1)
    hits = jnp.zeros((8, V), jnp.float32)
    for y in range(NY):
        for pay in (own_pay, other_pay):
            hits = hits + (pay[y, 4 * CAP:4 * CAP + 8, :] == w.astype(jnp.float32)).astype(jnp.float32)
    times = hits[:1, :128] + hits[:1, 128:] + (u == w).astype(jnp.float32)
    times = jnp.concatenate([times, times], axis=1)
    for copy in own_copies:
        copy.wait()
    for j in range(OCC_DEV):
        cols = slice(j * V, (j + 1) * V)
        coulomb = dot3(own_hi[...], own_lo[...], w_hi[:, cols], w_lo[:, cols])
        for i in range(OCC_DEV):
            c = coulomb[i * V:(i + 1) * V, :]
            scale = times / ((occ[2 * u + i] + occ[2 * w + j]) - virt_sum)
            hi, lo = split_hi_lo((2.0 * c.T - c) * scale)
            x_hi[cols, i * V:(i + 1) * V] = hi
            x_lo[cols, i * V:(i + 1) * V] = lo

    for k, out in enumerate(outs):
        for half in range(2):
            part = slice(k * 512 + half * 256, k * 512 + half * 256 + 256)
            term = dot3(w_hi[part, :], w_lo[part, :], x_hi[...], x_lo[...])
            for q in range(4):
                for i in range(OCC_DEV):
                    value = term[q * BLK:(q + 1) * BLK, i * V:(i + 1) * V]
                    if not first:
                        value = value + before[k][half * 4 + q, i]
                    out[half * 4 + q, i] = value


def per_device(three_center, counts, occ_energy, virt_energy, match_tables):
    y, c = lax.axis_index("y"), lax.axis_index("c")
    z, x = lax.axis_index("z"), lax.axis_index("x")
    grp, pos = y * NC + c, z * NX + x
    place = jnp.stack([c, pos, grp, z]).astype(jnp.int32)

    axes = ("y", "c", "z", "x")
    got = []
    for t in range(2):
        to = lax.rem(grp - pos + 32, 16) + 16 * lax.rem(pos // 16 + t, 2)
        piece = lax.dynamic_slice_in_dim(three_center, OCC_DEV * to, OCC_DEV, 0)
        perm = [
            (g * 32 + s, g * 32 + (g - s) % 16 + 16 * ((s // 16 + t) % 2))
            for g in range(16) for s in range(32)
        ]
        got.append(lax.ppermute(piece, axes, perm).reshape(OCC_DEV * CAP, V))

    both = lax.dynamic_slice_in_dim(three_center, 4 * grp, 4, 0).reshape(2, OCC_DEV, CAP, V)
    both = lax.all_gather(both, "x", axis=1)
    first_rows = lax.all_gather(both[0], "z")

    partners = lax.dynamic_slice_in_dim(match_tables[:, 0, :], pos, 1, 1).astype(jnp.float32)
    note = jnp.broadcast_to(jnp.repeat(partners.reshape(1, 2), 128, axis=1), (8, V))
    load = jnp.concatenate(got + [note], axis=0)
    sent = jnp.broadcast_to(load[None], (NY, 4 * CAP + 8, V))
    own_pay = lax.all_to_all(sent, "y", split_axis=0, concat_axis=0, tiled=True)

    def along_z(a, d):
        return lax.ppermute(a, "z", [(k, (k + d) % NZ) for k in range(NZ)])

    up, down = [both[1]], [both[1]]
    for step in range(3):
        up.append(along_z(up[-1], 1))
        down.append(along_z(down[-1], -1))
        if step == 1:
            own_pay, up[2], down[2] = lax.optimization_barrier((own_pay, up[2], down[2]))
    far = (along_z(up[3][:, :1], 1), along_z(down[3][:, 1:], -1))
    second_rows = (*up, *down[1:], *far)

    other_pay = lax.ppermute(own_pay, "c", [(0, 1), (1, 0)])

    smem = pl.BlockSpec(memory_space=pltpu.SMEM)
    vmem = pl.BlockSpec(memory_space=pltpu.VMEM)
    hbm = pl.BlockSpec(memory_space=pltpu.HBM)
    own_hi, own_lo = pl.pallas_call(
        own_rows_kernel,
        out_shape=[jax.ShapeDtypeStruct((OCC_DEV * V, NAUX), jnp.bfloat16)] * 2,
        in_specs=[smem, smem, vmem, vmem],
        out_specs=[hbm, hbm],
        scratch_shapes=[
            pltpu.VMEM((NAUX + PAD, OCC_DEV * V), jnp.float32),
            pltpu.VMEM((OCC_DEV * V, NAUX), jnp.bfloat16),
            pltpu.VMEM((OCC_DEV * V, NAUX), jnp.bfloat16),
            pltpu.SemaphoreType.DMA((2,)),
        ],
        compiler_params=pltpu.CompilerParams(vmem_limit_bytes=60 * MIB),
        name="own_rows",
    )(place, counts, own_pay, other_pay)

    part = jax.ShapeDtypeStruct((NY, OCC_DEV, BLK, V), jnp.float32)
    outs = ()
    for first, wide in ((True, (first_rows,)), (False, second_rows)):
        wide_dims = 2 * V
        outs = pl.pallas_call(
            functools.partial(block_kernel, first),
            out_shape=[part, part],
            in_specs=[smem] * 3 + [hbm] * 2 + [vmem] * 3 + [hbm] * len(wide) + [vmem] * len(outs),
            out_specs=[vmem, vmem],
            scratch_shapes=[
                pltpu.VMEM((OCC_DEV * V, NAUX), jnp.bfloat16),
                pltpu.VMEM((OCC_DEV * V, NAUX), jnp.bfloat16),
                pltpu.VMEM((NZ, NX, OCC_DEV, CAP, V), jnp.float32),
                pltpu.VMEM((NAUX + PAD, wide_dims), jnp.float32),
                pltpu.VMEM((NAUX, wide_dims), jnp.bfloat16),
                pltpu.VMEM((NAUX, wide_dims), jnp.bfloat16),
                pltpu.VMEM((wide_dims, OCC_DEV * V), jnp.bfloat16),
                pltpu.VMEM((wide_dims, OCC_DEV * V), jnp.bfloat16),
                pltpu.SemaphoreType.DMA((12,)),
            ],
            compiler_params=pltpu.CompilerParams(vmem_limit_bytes=60 * MIB),
            cost_estimate=pl.CostEstimate(flops=6 * 2 * 512 * 512 * 1024, bytes_accessed=8 * MIB, transcendentals=0),
            name="first_block" if first else "second_block",
        )(place, counts, occ_energy, own_hi, own_lo, own_pay, other_pay,
          virt_energy.reshape(1, V), *wide, *outs)
    theirs, mine = outs

    mine = mine + lax.ppermute(theirs, "c", [(0, 1), (1, 0)])
    pieces = lax.all_to_all(mine, "y", split_axis=0, concat_axis=0, tiled=True)
    return jnp.sum(pieces, axis=0)


def solution(mesh):
    fine = Mesh(np.asarray(mesh.devices).reshape(NY, NC, NZ, NX), ("y", "c", "z", "x"))
    wide, grp = ("z", "x"), ("y", "c")
    placed = (P(None, wide, None), P(), P(), P(), P(None, grp, None))
    return jax.shard_map(
        per_device, mesh=fine, in_specs=placed, out_specs=P(wide, grp, None), check_vma=False
    )
```

```python
import jax
import jax.numpy as jnp
import numpy as np
from jax import lax
from jax.experimental import pallas as pl
from jax.experimental.pallas import tpu as pltpu
from jax.sharding import Mesh, PartitionSpec as P

NAUX = 1024
OCC_DEV = 2
CAP = 40
V = 256
NY, NC, NZ, NX = 8, 2, 8, 4
BLK = 64
PAD = 48
MIB = 1 << 20


def split_hi_lo(x):
    hi = x.astype(jnp.bfloat16)
    lo = (x - hi.astype(jnp.float32)).astype(jnp.bfloat16)
    return hi, lo


def dot3(ah, al, bh, bl):
    def mm(a, b):
        return lax.dot_general(a, b, (((1,), (0,)), ((), ())), preferred_element_type=jnp.float32)

    return mm(ah, bh) + mm(ah, bl) + mm(al, bh)


def put_rows(dense, off, cols, block):
    base = pl.multiple_of(off // 8 * 8, 8)
    shift = off - base
    before = lax.broadcasted_iota(jnp.int32, (8, block.shape[1]), 0) < shift
    held = dense[pl.ds(base, 8), cols]
    for k in range(CAP // 8):
        turned = pltpu.roll(block[k * 8:(k + 1) * 8, :], shift, 0)
        dense[pl.ds(base + k * 8, 8), cols] = jnp.where(before, held, turned)
        held = turned
    dense[pl.ds(base + CAP, 8), cols] = held


def own_rows_kernel(place, counts, own_ref, other_ref, hi_ref, lo_ref, times_ref, dense):
    core, u, grp = place[0], place[1], place[2]
    for w in range(2):
        block = (2 * grp + w).astype(jnp.float32)
        hits = jnp.zeros((8, V), jnp.float32)
        for y in range(NY):
            for pay in (own_ref, other_ref):
                hits = hits + (pay[y, 4 * CAP:4 * CAP + 8, :] == block).astype(jnp.float32)
        times = hits[:, :128] + hits[:, 128:] + (u == 2 * grp + w).astype(jnp.float32)
        times_ref[w] = jnp.concatenate([times, times], axis=1)

    def put(s, off):
        g = lax.rem(s + u, 16)
        t = lax.rem(s // 16 + u // 16, 2)
        y = g // 2

        def copy(ref):
            for i in range(OCC_DEV):
                rows = ref[y, pl.ds(pl.multiple_of((t * OCC_DEV + i) * CAP, 8), CAP), :]
                put_rows(dense, off, slice(i * V, (i + 1) * V), rows)

        @pl.when(lax.rem(g, 2) == core)
        def _():
            copy(own_ref)

        @pl.when(lax.rem(g, 2) != core)
        def _():
            copy(other_ref)

        return off + counts[s]

    lax.fori_loop(0, 32, put, jnp.int32(0))

    def turn(n, carry):
        k, pair = n // 4, n % 4
        first = pl.multiple_of((4 * pair + lax.rem(core + 1 + k, 2)) * BLK, BLK)
        rows = jnp.concatenate(
            [dense[pl.ds(first, BLK), :], dense[pl.ds(first + 2 * BLK, BLK), :]], axis=0
        )
        hi, lo = split_hi_lo(rows.T)
        hi_ref[:, n * 128:(n + 1) * 128] = hi
        lo_ref[:, n * 128:(n + 1) * 128] = lo
        return carry

    for n in range(8):
        turn(n, 0)


def pair_kernel(place, counts, occ, own_hi_any, own_lo_any, times, virt, wide_any,
                theirs_ref, mine_ref, own_hi, own_lo, rows, dense, w_hi, w_lo, x_hi, x_lo, sems):
    core, u, grp = place[0], place[1], place[2]
    row_copies = [pltpu.make_async_copy(wide_any.at[z], rows.at[z], sems.at[z]) for z in range(NZ)]
    own_copies = [
        pltpu.make_async_copy(own_hi_any, own_hi, sems.at[NZ]),
        pltpu.make_async_copy(own_lo_any, own_lo, sems.at[NZ + 1]),
    ]
    for copy in row_copies + own_copies:
        copy.start()

    off = jnp.int32(0)
    for z in range(NZ):
        row_copies[z].wait()
        for x in range(NX):
            for j in range(4):
                put_rows(dense, off, slice(j * V, (j + 1) * V), rows[z, x, j])
            off = off + counts[z * NX + x]

    for k in range(2):
        for y in range(NY):
            src = pl.multiple_of((2 * y + lax.rem(core + 1 + k, 2)) * BLK, BLK)
            dst = slice((k * NY + y) * BLK, (k * NY + y + 1) * BLK)
            hi, lo = split_hi_lo(dense[pl.ds(src, BLK), :])
            w_hi[dst, :] = hi
            w_lo[dst, :] = lo

    virt_row = jnp.broadcast_to(virt[...], (V, V))
    virt_sum = virt_row + virt_row.T
    for copy in own_copies:
        copy.wait()
    for j in range(4):
        cols = slice(j * V, (j + 1) * V)
        coulomb = dot3(own_hi[...], own_lo[...], w_hi[:, cols], w_lo[:, cols])
        for i in range(OCC_DEV):
            c = coulomb[i * V:(i + 1) * V, :]
            scale = times[j // 2, :1, :] / ((occ[2 * u + i] + occ[4 * grp + j]) - virt_sum)
            hi, lo = split_hi_lo((2.0 * c.T - c) * scale)
            x_hi[cols, i * V:(i + 1) * V] = hi
            x_lo[cols, i * V:(i + 1) * V] = lo

    for k, out in enumerate((theirs_ref, mine_ref)):
        for half in range(2):
            rows = slice(k * 512 + half * 256, k * 512 + half * 256 + 256)
            term = dot3(w_hi[rows, :], w_lo[rows, :], x_hi[...], x_lo[...])
            for q in range(4):
                for i in range(OCC_DEV):
                    out[half * 4 + q, i] = term[q * BLK:(q + 1) * BLK, i * V:(i + 1) * V]


SMEM = pl.BlockSpec(memory_space=pltpu.SMEM)
VMEM = pl.BlockSpec(memory_space=pltpu.VMEM)
HBM = pl.BlockSpec(memory_space=pl.ANY)


def own_rows(place, counts, own_pay, other_pay):
    return pl.pallas_call(
        own_rows_kernel,
        out_shape=[jax.ShapeDtypeStruct((OCC_DEV * V, NAUX), jnp.bfloat16)] * 2
        + [jax.ShapeDtypeStruct((2, 8, V), jnp.float32)],
        in_specs=[SMEM, SMEM, VMEM, VMEM],
        out_specs=[VMEM] * 3,
        scratch_shapes=[pltpu.VMEM((NAUX + PAD, OCC_DEV * V), jnp.float32)],
        compiler_params=pltpu.CompilerParams(vmem_limit_bytes=24 * MIB),
        name="own_rows",
    )(place, counts, own_pay, other_pay)


def pairs(place, counts, occ_energy, own_hi, own_lo, times, virt, wide_all):
    part = jax.ShapeDtypeStruct((NY, OCC_DEV, BLK, V), jnp.float32)
    return pl.pallas_call(
        pair_kernel,
        out_shape=[part, part],
        in_specs=[SMEM] * 3 + [HBM, HBM, VMEM, VMEM, HBM],
        out_specs=[VMEM, VMEM],
        scratch_shapes=[
            pltpu.VMEM((OCC_DEV * V, NAUX), jnp.bfloat16),
            pltpu.VMEM((OCC_DEV * V, NAUX), jnp.bfloat16),
            pltpu.VMEM((NZ, NX, 4, CAP, V), jnp.float32),
            pltpu.VMEM((NAUX + PAD, 4 * V), jnp.float32),
            pltpu.VMEM((NAUX, 4 * V), jnp.bfloat16),
            pltpu.VMEM((NAUX, 4 * V), jnp.bfloat16),
            pltpu.VMEM((4 * V, OCC_DEV * V), jnp.bfloat16),
            pltpu.VMEM((4 * V, OCC_DEV * V), jnp.bfloat16),
            pltpu.SemaphoreType.DMA((NZ + 2,)),
        ],
        compiler_params=pltpu.CompilerParams(vmem_limit_bytes=56 * MIB),
        name="pairs",
    )(place, counts, occ_energy, own_hi, own_lo, times, virt, wide_all)


def per_device(three_center, counts, occ_energy, virt_energy, match_tables):
    y, c = lax.axis_index("y"), lax.axis_index("c")
    z, x = lax.axis_index("z"), lax.axis_index("x")
    grp, pos = y * NC + c, z * NX + x
    place = jnp.stack([c, pos, grp]).astype(jnp.int32)

    wide_part = lax.dynamic_slice_in_dim(three_center, 4 * grp, 4, 0)
    wide_all = lax.all_gather(lax.all_gather(wide_part, "x"), "z")

    axes = ("y", "c", "z", "x")
    got = []
    for t in range(2):
        to = lax.rem(grp - pos + 32, 16) + 16 * lax.rem(pos // 16 + t, 2)
        piece = lax.dynamic_slice_in_dim(three_center, OCC_DEV * to, OCC_DEV, 0)
        perm = [
            (g * 32 + s, g * 32 + (g - s) % 16 + 16 * ((s // 16 + t) % 2))
            for g in range(16) for s in range(32)
        ]
        got.append(lax.ppermute(piece, axes, perm).reshape(OCC_DEV * CAP, V))
    partners = lax.dynamic_slice_in_dim(match_tables[:, 0, :], pos, 1, 1).astype(jnp.float32)
    note = jnp.broadcast_to(jnp.repeat(partners.reshape(1, 2), 128, axis=1), (8, V))
    load = jnp.concatenate(got + [note], axis=0)
    sent = jnp.broadcast_to(load[None], (NY, 4 * CAP + 8, V))
    own_pay = lax.all_to_all(sent, "y", split_axis=0, concat_axis=0, tiled=True)
    other_pay = lax.ppermute(own_pay, "c", [(0, 1), (1, 0)])

    own_hi, own_lo, times = own_rows(place, counts, own_pay, other_pay)
    theirs, mine = pairs(place, counts, occ_energy, own_hi, own_lo, times, virt_energy.reshape(1, V), wide_all)

    mine = mine + lax.ppermute(theirs, "c", [(0, 1), (1, 0)])
    pieces = lax.all_to_all(mine, "y", split_axis=0, concat_axis=0, tiled=True)
    return jnp.sum(pieces, axis=0)


def solution(mesh):
    fine = Mesh(np.asarray(mesh.devices).reshape(NY, NC, NZ, NX), ("y", "c", "z", "x"))
    wide, grp = ("z", "x"), ("y", "c")
    placed = (P(None, wide, None), P(), P(), P(), P(None, grp, None))
    return jax.shard_map(
        per_device, mesh=fine, in_specs=placed, out_specs=P(wide, grp, None), check_vma=False
    )
```

```python
import jax
import jax.numpy as jnp
import numpy as np
from jax import lax
from jax.experimental import pallas as pl
from jax.experimental.pallas import tpu as pltpu
from jax.sharding import Mesh, PartitionSpec as P

NAUX = 1024
OCC_DEV = 2
CAP = 40
V = 256
NY, NC, NZ, NX = 8, 2, 8, 4
BLK = 64
PAD = 48
MIB = 1 << 20


def split_hi_lo(x):
    hi = x.astype(jnp.bfloat16)
    lo = (x - hi.astype(jnp.float32)).astype(jnp.bfloat16)
    return hi, lo


def dot3(ah, al, bh, bl):
    def mm(a, b):
        return lax.dot_general(a, b, (((1,), (0,)), ((), ())), preferred_element_type=jnp.float32)

    return mm(ah, bh) + mm(ah, bl) + mm(al, bh)


def put_rows(dense, off, cols, block):
    base = pl.multiple_of(off // 8 * 8, 8)
    shift = off - base
    before = lax.broadcasted_iota(jnp.int32, (8, block.shape[1]), 0) < shift
    held = dense[pl.ds(base, 8), cols]
    for k in range(CAP // 8):
        turned = pltpu.roll(block[k * 8:(k + 1) * 8, :], shift, 0)
        dense[pl.ds(base + k * 8, 8), cols] = jnp.where(before, held, turned)
        held = turned
    dense[pl.ds(base + CAP, 8), cols] = held


def own_rows_kernel(place, counts, own_ref, other_ref, hi_ref, lo_ref, times_ref, dense):
    core, u, grp = place[0], place[1], place[2]
    for w in range(2):
        block = (2 * grp + w).astype(jnp.float32)
        hits = jnp.zeros((8, V), jnp.float32)
        for y in range(NY):
            for pay in (own_ref, other_ref):
                hits = hits + (pay[y, 4 * CAP:4 * CAP + 8, :] == block).astype(jnp.float32)
        times = hits[:, :128] + hits[:, 128:] + (u == 2 * grp + w).astype(jnp.float32)
        times_ref[w] = jnp.concatenate([times, times], axis=1)

    def put(s, off):
        g = lax.rem(s + u, 16)
        t = lax.rem(s // 16 + u // 16, 2)
        y = g // 2

        def copy(ref):
            for i in range(OCC_DEV):
                rows = ref[y, pl.ds(pl.multiple_of((t * OCC_DEV + i) * CAP, 8), CAP), :]
                put_rows(dense, off, slice(i * V, (i + 1) * V), rows)

        @pl.when(lax.rem(g, 2) == core)
        def _():
            copy(own_ref)

        @pl.when(lax.rem(g, 2) != core)
        def _():
            copy(other_ref)

        return off + counts[s]

    lax.fori_loop(0, 32, put, jnp.int32(0))

    def turn(n, carry):
        k, pair = n // 4, n % 4
        first = pl.multiple_of((4 * pair + lax.rem(core + 1 + k, 2)) * BLK, BLK)
        rows = jnp.concatenate(
            [dense[pl.ds(first, BLK), :], dense[pl.ds(first + 2 * BLK, BLK), :]], axis=0
        )
        hi, lo = split_hi_lo(rows.T)
        hi_ref[:, n * 128:(n + 1) * 128] = hi
        lo_ref[:, n * 128:(n + 1) * 128] = lo
        return carry

    for n in range(8):
        turn(n, 0)


def pair_kernel(place, counts, occ, own_hi_any, own_lo_any, times, virt, wide_any,
                theirs_ref, mine_ref, own_hi, own_lo, rows, dense, w_hi, w_lo, x_hi, x_lo, sems):
    core, u, grp = place[0], place[1], place[2]
    row_copies = [pltpu.make_async_copy(wide_any.at[z], rows.at[z], sems.at[z]) for z in range(NZ)]
    own_copies = [
        pltpu.make_async_copy(own_hi_any, own_hi, sems.at[NZ]),
        pltpu.make_async_copy(own_lo_any, own_lo, sems.at[NZ + 1]),
    ]
    for copy in row_copies + own_copies:
        copy.start()

    off = jnp.int32(0)
    for z in range(NZ):
        row_copies[z].wait()
        for x in range(NX):
            for j in range(4):
                put_rows(dense, off, slice(j * V, (j + 1) * V), rows[z, x, j])
            off = off + counts[z * NX + x]

    for k in range(2):
        for y in range(NY):
            src = pl.multiple_of((2 * y + lax.rem(core + 1 + k, 2)) * BLK, BLK)
            dst = slice((k * NY + y) * BLK, (k * NY + y + 1) * BLK)
            hi, lo = split_hi_lo(dense[pl.ds(src, BLK), :])
            w_hi[dst, :] = hi
            w_lo[dst, :] = lo

    virt_row = jnp.broadcast_to(virt[...], (V, V))
    virt_sum = virt_row + virt_row.T
    for copy in own_copies:
        copy.wait()
    for j in range(4):
        cols = slice(j * V, (j + 1) * V)
        coulomb = dot3(own_hi[...], own_lo[...], w_hi[:, cols], w_lo[:, cols])
        for i in range(OCC_DEV):
            c = coulomb[i * V:(i + 1) * V, :]
            scale = times[j // 2, :1, :] / ((occ[2 * u + i] + occ[4 * grp + j]) - virt_sum)
            hi, lo = split_hi_lo((2.0 * c.T - c) * scale)
            x_hi[cols, i * V:(i + 1) * V] = hi
            x_lo[cols, i * V:(i + 1) * V] = lo

    for k, out in enumerate((theirs_ref, mine_ref)):
        part = slice(k * 512, (k + 1) * 512)
        for i in range(OCC_DEV):
            cols = slice(i * V, (i + 1) * V)
            term = dot3(w_hi[part, :], w_lo[part, :], x_hi[:, cols], x_lo[:, cols])
            for q in range(NY):
                out[q, i] = term[q * BLK:(q + 1) * BLK, :]


SMEM = pl.BlockSpec(memory_space=pltpu.SMEM)
VMEM = pl.BlockSpec(memory_space=pltpu.VMEM)
HBM = pl.BlockSpec(memory_space=pl.ANY)


def own_rows(place, counts, own_pay, other_pay):
    return pl.pallas_call(
        own_rows_kernel,
        out_shape=[jax.ShapeDtypeStruct((OCC_DEV * V, NAUX), jnp.bfloat16)] * 2
        + [jax.ShapeDtypeStruct((2, 8, V), jnp.float32)],
        in_specs=[SMEM, SMEM, VMEM, VMEM],
        out_specs=[VMEM] * 3,
        scratch_shapes=[pltpu.VMEM((NAUX + PAD, OCC_DEV * V), jnp.float32)],
        compiler_params=pltpu.CompilerParams(vmem_limit_bytes=24 * MIB),
        name="own_rows",
    )(place, counts, own_pay, other_pay)


def pairs(place, counts, occ_energy, own_hi, own_lo, times, virt, wide_all):
    part = jax.ShapeDtypeStruct((NY, OCC_DEV, BLK, V), jnp.float32)
    return pl.pallas_call(
        pair_kernel,
        out_shape=[part, part],
        in_specs=[SMEM] * 3 + [HBM, HBM, VMEM, VMEM, HBM],
        out_specs=[VMEM, VMEM],
        scratch_shapes=[
            pltpu.VMEM((OCC_DEV * V, NAUX), jnp.bfloat16),
            pltpu.VMEM((OCC_DEV * V, NAUX), jnp.bfloat16),
            pltpu.VMEM((NZ, NX, 4, CAP, V), jnp.float32),
            pltpu.VMEM((NAUX + PAD, 4 * V), jnp.float32),
            pltpu.VMEM((NAUX, 4 * V), jnp.bfloat16),
            pltpu.VMEM((NAUX, 4 * V), jnp.bfloat16),
            pltpu.VMEM((4 * V, OCC_DEV * V), jnp.bfloat16),
            pltpu.VMEM((4 * V, OCC_DEV * V), jnp.bfloat16),
            pltpu.SemaphoreType.DMA((NZ + 2,)),
        ],
        compiler_params=pltpu.CompilerParams(vmem_limit_bytes=48 * MIB),
        name="pairs",
    )(place, counts, occ_energy, own_hi, own_lo, times, virt, wide_all)


def per_device(three_center, counts, occ_energy, virt_energy, match_tables):
    y, c = lax.axis_index("y"), lax.axis_index("c")
    z, x = lax.axis_index("z"), lax.axis_index("x")
    grp, pos = y * NC + c, z * NX + x
    place = jnp.stack([c, pos, grp]).astype(jnp.int32)

    wide_part = lax.dynamic_slice_in_dim(three_center, 4 * grp, 4, 0)
    wide_all = lax.all_gather(lax.all_gather(wide_part, "x"), "z")

    axes = ("y", "c", "z", "x")
    got = []
    for t in range(2):
        to = lax.rem(grp - pos + 32, 16) + 16 * lax.rem(pos // 16 + t, 2)
        piece = lax.dynamic_slice_in_dim(three_center, OCC_DEV * to, OCC_DEV, 0)
        perm = [
            (g * 32 + s, g * 32 + (g - s) % 16 + 16 * ((s // 16 + t) % 2))
            for g in range(16) for s in range(32)
        ]
        got.append(lax.ppermute(piece, axes, perm).reshape(OCC_DEV * CAP, V))
    partners = lax.dynamic_slice_in_dim(match_tables[:, 0, :], pos, 1, 1).astype(jnp.float32)
    note = jnp.broadcast_to(jnp.repeat(partners.reshape(1, 2), 128, axis=1), (8, V))
    load = jnp.concatenate(got + [note], axis=0)
    sent = jnp.broadcast_to(load[None], (NY, 4 * CAP + 8, V))
    own_pay = lax.all_to_all(sent, "y", split_axis=0, concat_axis=0, tiled=True)
    other_pay = lax.ppermute(own_pay, "c", [(0, 1), (1, 0)])

    own_hi, own_lo, times = own_rows(place, counts, own_pay, other_pay)
    theirs, mine = pairs(place, counts, occ_energy, own_hi, own_lo, times, virt_energy.reshape(1, V), wide_all)

    mine = mine + lax.ppermute(theirs, "c", [(0, 1), (1, 0)])
    pieces = lax.all_to_all(mine, "y", split_axis=0, concat_axis=0, tiled=True)
    return jnp.sum(pieces, axis=0)


def solution(mesh):
    fine = Mesh(np.asarray(mesh.devices).reshape(NY, NC, NZ, NX), ("y", "c", "z", "x"))
    wide, grp = ("z", "x"), ("y", "c")
    placed = (P(None, wide, None), P(), P(), P(), P(None, grp, None))
    return jax.shard_map(
        per_device, mesh=fine, in_specs=placed, out_specs=P(wide, grp, None), check_vma=False
    )
```

```python
import jax
import jax.numpy as jnp
import numpy as np
from jax import lax
from jax.experimental import pallas as pl
from jax.experimental.pallas import tpu as pltpu
from jax.sharding import Mesh, PartitionSpec as P

NAUX = 1024
OCC_DEV = 2
CAP = 40
V = 256
NY, NC, NZ, NX = 8, 2, 8, 4
BLK = 64
PAD = 48
MIB = 1 << 20


def split_hi_lo(x):
    hi = x.astype(jnp.bfloat16)
    lo = (x - hi.astype(jnp.float32)).astype(jnp.bfloat16)
    return hi, lo


def dot3(ah, al, bh, bl):
    def mm(a, b):
        return lax.dot_general(a, b, (((1,), (0,)), ((), ())), preferred_element_type=jnp.float32)

    return mm(ah, bh) + mm(ah, bl) + mm(al, bh)


def put_rows(dense, off, cols, block):
    base = pl.multiple_of(off // 8 * 8, 8)
    shift = off - base
    before = lax.broadcasted_iota(jnp.int32, (8, block.shape[1]), 0) < shift
    held = dense[pl.ds(base, 8), cols]
    for k in range(CAP // 8):
        turned = pltpu.roll(block[k * 8:(k + 1) * 8, :], shift, 0)
        dense[pl.ds(base + k * 8, 8), cols] = jnp.where(before, held, turned)
        held = turned
    dense[pl.ds(base + CAP, 8), cols] = held


def own_rows_kernel(place, counts, own_ref, hi_ref, lo_ref, times_ref, dense):
    core, u, grp = place[0], place[1], place[2]
    for w in range(2):
        block = (2 * grp + w).astype(jnp.float32)
        hits = jnp.zeros((8, V), jnp.float32)
        for g in range(NY * NC):
            hits = hits + (own_ref[g, 4 * CAP:4 * CAP + 8, :] == block).astype(jnp.float32)
        times = hits[:, :128] + hits[:, 128:] + (u == 2 * grp + w).astype(jnp.float32)
        times_ref[w] = jnp.concatenate([times, times], axis=1)

    def put(s, off):
        g = lax.rem(s + u, 16)
        t = lax.rem(s // 16 + u // 16, 2)
        for i in range(OCC_DEV):
            rows = own_ref[g, pl.ds(pl.multiple_of((t * OCC_DEV + i) * CAP, 8), CAP), :]
            put_rows(dense, off, slice(i * V, (i + 1) * V), rows)
        return off + counts[s]

    lax.fori_loop(0, 32, put, jnp.int32(0))

    def turn(n, carry):
        k, pair = n // 4, n % 4
        first = pl.multiple_of((4 * pair + lax.rem(core + 1 + k, 2)) * BLK, BLK)
        rows = jnp.concatenate(
            [dense[pl.ds(first, BLK), :], dense[pl.ds(first + 2 * BLK, BLK), :]], axis=0
        )
        hi, lo = split_hi_lo(rows.T)
        hi_ref[:, n * 128:(n + 1) * 128] = hi
        lo_ref[:, n * 128:(n + 1) * 128] = lo
        return carry

    for n in range(8):
        turn(n, 0)


def pair_kernel(place, counts, occ, own_hi_any, own_lo_any, times, virt, *refs):
    parts, refs = refs[:2 * NZ], refs[2 * NZ:]
    theirs_ref, mine_ref, own_hi, own_lo, rows, dense, w_hi, w_lo, x_hi, x_lo, sems = refs
    core, u, grp = place[0], place[1], place[2]
    z_here = place[3]

    def copies_of(refs, d, js, first_sem):
        at = lax.rem(z_here + d + NZ, NZ)
        return [
            pltpu.make_async_copy(ref, rows.at[at, :, pl.ds(2 * j, 2)], sems.at[first_sem + n])
            for n, (ref, j) in enumerate(zip(refs, js))
        ]

    row_copies = []
    for n, d in enumerate((0, -1, -2, -3, 1, 2, 3, 4)):
        row_copies += copies_of(parts[2 * n:2 * n + 2], d, (0, 1), 2 + 2 * n)
    own_copies = [
        pltpu.make_async_copy(own_hi_any, own_hi, sems.at[0]),
        pltpu.make_async_copy(own_lo_any, own_lo, sems.at[1]),
    ]
    for copy in row_copies + own_copies:
        copy.start()

    for copy in row_copies:
        copy.wait()
    off = jnp.int32(0)
    for z in range(NZ):
        for x in range(NX):
            for j in range(4):
                put_rows(dense, off, slice(j * V, (j + 1) * V), rows[z, x, j])
            off = off + counts[z * NX + x]

    for k in range(2):
        for y in range(NY):
            src = pl.multiple_of((2 * y + lax.rem(core + 1 + k, 2)) * BLK, BLK)
            dst = slice((k * NY + y) * BLK, (k * NY + y + 1) * BLK)
            hi, lo = split_hi_lo(dense[pl.ds(src, BLK), :])
            w_hi[dst, :] = hi
            w_lo[dst, :] = lo

    virt_row = jnp.broadcast_to(virt[...], (V, V))
    virt_sum = virt_row + virt_row.T
    for copy in own_copies:
        copy.wait()
    for j in range(4):
        cols = slice(j * V, (j + 1) * V)
        coulomb = dot3(own_hi[...], own_lo[...], w_hi[:, cols], w_lo[:, cols])
        for i in range(OCC_DEV):
            c = coulomb[i * V:(i + 1) * V, :]
            scale = times[j // 2, :1, :] / ((occ[2 * u + i] + occ[4 * grp + j]) - virt_sum)
            hi, lo = split_hi_lo((2.0 * c.T - c) * scale)
            x_hi[cols, i * V:(i + 1) * V] = hi
            x_lo[cols, i * V:(i + 1) * V] = lo

    for k, out in enumerate((theirs_ref, mine_ref)):
        part = slice(k * 512, (k + 1) * 512)
        for i in range(OCC_DEV):
            cols = slice(i * V, (i + 1) * V)
            term = dot3(w_hi[part, :], w_lo[part, :], x_hi[:, cols], x_lo[:, cols])
            for q in range(NY):
                out[q, i] = term[q * BLK:(q + 1) * BLK, :]


SMEM = pl.BlockSpec(memory_space=pltpu.SMEM)
VMEM = pl.BlockSpec(memory_space=pltpu.VMEM)
HBM = pl.BlockSpec(memory_space=pl.ANY)


def own_rows(place, counts, own_pay):
    return pl.pallas_call(
        own_rows_kernel,
        out_shape=[jax.ShapeDtypeStruct((OCC_DEV * V, NAUX), jnp.bfloat16)] * 2
        + [jax.ShapeDtypeStruct((2, 8, V), jnp.float32)],
        in_specs=[SMEM, SMEM, VMEM],
        out_specs=[VMEM] * 3,
        scratch_shapes=[pltpu.VMEM((NAUX + PAD, OCC_DEV * V), jnp.float32)],
        compiler_params=pltpu.CompilerParams(vmem_limit_bytes=24 * MIB),
        name="own_rows",
    )(place, counts, own_pay)


def pairs(place, counts, occ_energy, own_hi, own_lo, times, virt, parts):
    part = jax.ShapeDtypeStruct((NY, OCC_DEV, BLK, V), jnp.float32)
    return pl.pallas_call(
        pair_kernel,
        out_shape=[part, part],
        in_specs=[SMEM] * 3 + [HBM, HBM, VMEM, VMEM] + [HBM] * (2 * NZ),
        out_specs=[VMEM, VMEM],
        scratch_shapes=[
            pltpu.VMEM((OCC_DEV * V, NAUX), jnp.bfloat16),
            pltpu.VMEM((OCC_DEV * V, NAUX), jnp.bfloat16),
            pltpu.VMEM((NZ, NX, 4, CAP, V), jnp.float32),
            pltpu.VMEM((NAUX + PAD, 4 * V), jnp.float32),
            pltpu.VMEM((NAUX, 4 * V), jnp.bfloat16),
            pltpu.VMEM((NAUX, 4 * V), jnp.bfloat16),
            pltpu.VMEM((4 * V, OCC_DEV * V), jnp.bfloat16),
            pltpu.VMEM((4 * V, OCC_DEV * V), jnp.bfloat16),
            pltpu.SemaphoreType.DMA((2 + 2 * NZ,)),
        ],
        compiler_params=pltpu.CompilerParams(vmem_limit_bytes=36 * MIB),
        name="pairs",
    )(place, counts, occ_energy, own_hi, own_lo, times, virt, *parts)


def per_device(three_center, counts, occ_energy, virt_energy, match_tables):
    y, c = lax.axis_index("y"), lax.axis_index("c")
    z, x = lax.axis_index("z"), lax.axis_index("x")
    grp, pos = y * NC + c, z * NX + x
    place = jnp.stack([c, pos, grp, z]).astype(jnp.int32)

    wide_part = lax.dynamic_slice_in_dim(three_center, 4 * grp, 4, 0).reshape(2, OCC_DEV, CAP, V)
    here = lax.all_gather(wide_part, "x", axis=1)

    axes = ("y", "c", "z", "x")
    three_center, here = lax.optimization_barrier((three_center, here))
    got = []
    for t in range(2):
        to = lax.rem(grp - pos + 32, 16) + 16 * lax.rem(pos // 16 + t, 2)
        piece = lax.dynamic_slice_in_dim(three_center, OCC_DEV * to, OCC_DEV, 0)
        perm = [
            (g * 32 + s, g * 32 + (g - s) % 16 + 16 * ((s // 16 + t) % 2))
            for g in range(16) for s in range(32)
        ]
        got.append(lax.ppermute(piece, axes, perm).reshape(OCC_DEV * CAP, V))
    partners = lax.dynamic_slice_in_dim(match_tables[:, 0, :], pos, 1, 1).astype(jnp.float32)
    note = jnp.broadcast_to(jnp.repeat(partners.reshape(1, 2), 128, axis=1), (8, V))
    load = jnp.concatenate(got + [note], axis=0)
    own_pay = lax.all_gather(load, ("y", "c"))

    def along_z(a, d):
        return lax.ppermute(a, "z", [(k, (k + d) % NZ) for k in range(NZ)])

    up, down = [[here[0], here[1]]], [[here[0], here[1]]]
    for _ in range(3):
        up.append([along_z(a, 1) for a in up[-1]])
        down.append([along_z(a, -1) for a in down[-1]])
    far = [along_z(up[3][0], 1), along_z(down[3][1], -1)]
    parts = sum(up + down[1:], []) + far

    own_hi, own_lo, times = own_rows(place, counts, own_pay)
    theirs, mine = pairs(place, counts, occ_energy, own_hi, own_lo, times, virt_energy.reshape(1, V), parts)

    mine = mine + lax.ppermute(theirs, "c", [(0, 1), (1, 0)])
    pieces = lax.all_to_all(mine, "y", split_axis=0, concat_axis=0, tiled=True)
    return jnp.sum(pieces, axis=0)


def solution(mesh):
    fine = Mesh(np.asarray(mesh.devices).reshape(NY, NC, NZ, NX), ("y", "c", "z", "x"))
    wide, grp = ("z", "x"), ("y", "c")
    placed = (P(None, wide, None), P(), P(), P(), P(None, grp, None))
    return jax.shard_map(
        per_device, mesh=fine, in_specs=placed, out_specs=P(wide, grp, None), check_vma=False
    )
```

```python
import jax
import jax.numpy as jnp
import numpy as np
from jax import lax
from jax.experimental import pallas as pl
from jax.experimental.pallas import tpu as pltpu
from jax.sharding import Mesh, PartitionSpec as P

NAUX = 1024
OCC_DEV = 2
CAP = 40
V = 256
NY, NC, NZ, NX = 8, 2, 8, 4
BLK = 64
PAD = 48
MIB = 1 << 20


def split_hi_lo(x):
    hi = x.astype(jnp.bfloat16)
    lo = (x - hi.astype(jnp.float32)).astype(jnp.bfloat16)
    return hi, lo


def dot3(ah, al, bh, bl):
    def mm(a, b):
        return lax.dot_general(a, b, (((1,), (0,)), ((), ())), preferred_element_type=jnp.float32)

    return mm(ah, bh) + mm(ah, bl) + mm(al, bh)


def put_rows(dense, off, cols, block):
    base = pl.multiple_of(off // 8 * 8, 8)
    shift = off - base
    before = lax.broadcasted_iota(jnp.int32, (8, block.shape[1]), 0) < shift
    held = dense[pl.ds(base, 8), cols]
    for k in range(CAP // 8):
        turned = pltpu.roll(block[k * 8:(k + 1) * 8, :], shift, 0)
        dense[pl.ds(base + k * 8, 8), cols] = jnp.where(before, held, turned)
        held = turned
    dense[pl.ds(base + CAP, 8), cols] = held


def own_rows_kernel(place, counts, own_ref, hi_ref, lo_ref, times_ref, dense):
    core, u, grp = place[0], place[1], place[2]
    for w in range(2):
        block = (2 * grp + w).astype(jnp.float32)
        hits = jnp.zeros((8, V), jnp.float32)
        for g in range(NY * NC):
            hits = hits + (own_ref[g, 4 * CAP:4 * CAP + 8, :] == block).astype(jnp.float32)
        times = hits[:, :128] + hits[:, 128:] + (u == 2 * grp + w).astype(jnp.float32)
        times_ref[w] = jnp.concatenate([times, times], axis=1)

    def put(s, off):
        g = lax.rem(s + u, 16)
        t = lax.rem(s // 16 + u // 16, 2)
        for i in range(OCC_DEV):
            rows = own_ref[g, pl.ds(pl.multiple_of((t * OCC_DEV + i) * CAP, 8), CAP), :]
            put_rows(dense, off, slice(i * V, (i + 1) * V), rows)
        return off + counts[s]

    lax.fori_loop(0, 32, put, jnp.int32(0))

    def turn(n, carry):
        k, pair = n // 4, n % 4
        first = pl.multiple_of((4 * pair + lax.rem(core + 1 + k, 2)) * BLK, BLK)
        rows = jnp.concatenate(
            [dense[pl.ds(first, BLK), :], dense[pl.ds(first + 2 * BLK, BLK), :]], axis=0
        )
        hi, lo = split_hi_lo(rows.T)
        hi_ref[:, n * 128:(n + 1) * 128] = hi
        lo_ref[:, n * 128:(n + 1) * 128] = lo
        return carry

    for n in range(8):
        turn(n, 0)


def pair_kernel(place, counts, occ, own_hi_any, own_lo_any, times, virt, *refs):
    parts, refs = refs[:2 * NZ], refs[2 * NZ:]
    theirs_ref, mine_ref, own_hi, own_lo, rows, dense, w_hi, w_lo, x_hi, x_lo, sems = refs
    core, u, grp = place[0], place[1], place[2]
    z_here = place[3]

    def copies_of(refs, d, js, first_sem):
        at = lax.rem(z_here + d + NZ, NZ)
        return [
            pltpu.make_async_copy(
                ref.at[e], rows.at[at, lax.rem(place[4] - e + NX, NX), pl.ds(2 * j, 2)],
                sems.at[first_sem + n * NX + e],
            )
            for n, (ref, j) in enumerate(zip(refs, js)) for e in range(NX)
        ]

    row_copies = []
    for n, d in enumerate((0, -1, -2, -3, 1, 2, 3, 4)):
        row_copies += copies_of(parts[2 * n:2 * n + 2], d, (0, 1), 2 + 2 * NX * n)
    own_copies = [
        pltpu.make_async_copy(own_hi_any, own_hi, sems.at[0]),
        pltpu.make_async_copy(own_lo_any, own_lo, sems.at[1]),
    ]
    for copy in row_copies + own_copies:
        copy.start()

    for copy in row_copies:
        copy.wait()
    off = jnp.int32(0)
    for z in range(NZ):
        for x in range(NX):
            for j in range(4):
                put_rows(dense, off, slice(j * V, (j + 1) * V), rows[z, x, j])
            off = off + counts[z * NX + x]

    for k in range(2):
        for y in range(NY):
            src = pl.multiple_of((2 * y + lax.rem(core + 1 + k, 2)) * BLK, BLK)
            dst = slice((k * NY + y) * BLK, (k * NY + y + 1) * BLK)
            hi, lo = split_hi_lo(dense[pl.ds(src, BLK), :])
            w_hi[dst, :] = hi
            w_lo[dst, :] = lo

    virt_row = jnp.broadcast_to(virt[...], (V, V))
    virt_sum = virt_row + virt_row.T
    for copy in own_copies:
        copy.wait()
    for j in range(4):
        cols = slice(j * V, (j + 1) * V)
        coulomb = dot3(own_hi[...], own_lo[...], w_hi[:, cols], w_lo[:, cols])
        for i in range(OCC_DEV):
            c = coulomb[i * V:(i + 1) * V, :]
            scale = times[j // 2, :1, :] / ((occ[2 * u + i] + occ[4 * grp + j]) - virt_sum)
            hi, lo = split_hi_lo((2.0 * c.T - c) * scale)
            x_hi[cols, i * V:(i + 1) * V] = hi
            x_lo[cols, i * V:(i + 1) * V] = lo

    for k, out in enumerate((theirs_ref, mine_ref)):
        part = slice(k * 512, (k + 1) * 512)
        for i in range(OCC_DEV):
            cols = slice(i * V, (i + 1) * V)
            term = dot3(w_hi[part, :], w_lo[part, :], x_hi[:, cols], x_lo[:, cols])
            for q in range(NY):
                out[q, i] = term[q * BLK:(q + 1) * BLK, :]


SMEM = pl.BlockSpec(memory_space=pltpu.SMEM)
VMEM = pl.BlockSpec(memory_space=pltpu.VMEM)
HBM = pl.BlockSpec(memory_space=pl.ANY)


def own_rows(place, counts, own_pay):
    return pl.pallas_call(
        own_rows_kernel,
        out_shape=[jax.ShapeDtypeStruct((OCC_DEV * V, NAUX), jnp.bfloat16)] * 2
        + [jax.ShapeDtypeStruct((2, 8, V), jnp.float32)],
        in_specs=[SMEM, SMEM, VMEM],
        out_specs=[VMEM] * 3,
        scratch_shapes=[pltpu.VMEM((NAUX + PAD, OCC_DEV * V), jnp.float32)],
        compiler_params=pltpu.CompilerParams(vmem_limit_bytes=24 * MIB),
        name="own_rows",
    )(place, counts, own_pay)


def pairs(place, counts, occ_energy, own_hi, own_lo, times, virt, parts):
    part = jax.ShapeDtypeStruct((NY, OCC_DEV, BLK, V), jnp.float32)
    return pl.pallas_call(
        pair_kernel,
        out_shape=[part, part],
        in_specs=[SMEM] * 3 + [HBM, HBM, VMEM, VMEM] + [HBM] * (2 * NZ),
        out_specs=[VMEM, VMEM],
        scratch_shapes=[
            pltpu.VMEM((OCC_DEV * V, NAUX), jnp.bfloat16),
            pltpu.VMEM((OCC_DEV * V, NAUX), jnp.bfloat16),
            pltpu.VMEM((NZ, NX, 4, CAP, V), jnp.float32),
            pltpu.VMEM((NAUX + PAD, 4 * V), jnp.float32),
            pltpu.VMEM((NAUX, 4 * V), jnp.bfloat16),
            pltpu.VMEM((NAUX, 4 * V), jnp.bfloat16),
            pltpu.VMEM((4 * V, OCC_DEV * V), jnp.bfloat16),
            pltpu.VMEM((4 * V, OCC_DEV * V), jnp.bfloat16),
            pltpu.SemaphoreType.DMA((2 + 2 * NZ * NX,)),
        ],
        compiler_params=pltpu.CompilerParams(vmem_limit_bytes=36 * MIB),
        name="pairs",
    )(place, counts, occ_energy, own_hi, own_lo, times, virt, *parts)


def per_device(three_center, counts, occ_energy, virt_energy, match_tables):
    y, c = lax.axis_index("y"), lax.axis_index("c")
    z, x = lax.axis_index("z"), lax.axis_index("x")
    grp, pos = y * NC + c, z * NX + x
    place = jnp.stack([c, pos, grp, z, x]).astype(jnp.int32)

    wide_part = lax.dynamic_slice_in_dim(three_center, 4 * grp, 4, 0)

    def along(a, axis, size, d):
        return lax.ppermute(a, axis, [(k, (k + d) % size) for k in range(size)])

    beside = [along(wide_part, "x", NX, d) for d in (1, 2, 3)]
    axes = ("y", "c", "z", "x")
    got = []
    for t in range(2):
        to = lax.rem(grp - pos + 32, 16) + 16 * lax.rem(pos // 16 + t, 2)
        piece = lax.dynamic_slice_in_dim(three_center, OCC_DEV * to, OCC_DEV, 0)
        perm = [
            (g * 32 + s, g * 32 + (g - s) % 16 + 16 * ((s // 16 + t) % 2))
            for g in range(16) for s in range(32)
        ]
        got.append(lax.ppermute(piece, axes, perm))
    got, beside = lax.optimization_barrier((got, beside))
    got = [a.reshape(OCC_DEV * CAP, V) for a in got]
    row = jnp.stack([wide_part] + beside)

    partners = lax.dynamic_slice_in_dim(match_tables[:, 0, :], pos, 1, 1).astype(jnp.float32)
    note = jnp.broadcast_to(jnp.repeat(partners.reshape(1, 2), 128, axis=1), (8, V))
    load = jnp.concatenate(got + [note], axis=0)
    own_pay = lax.all_gather(load, ("y", "c"))

    up, down = [[row[:, :2], row[:, 2:]]], [[row[:, :2], row[:, 2:]]]
    for _ in range(3):
        up.append([along(a, "z", NZ, 1) for a in up[-1]])
        down.append([along(a, "z", NZ, -1) for a in down[-1]])
    far = [along(up[3][0], "z", NZ, 1), along(down[3][1], "z", NZ, -1)]
    parts = sum(up + down[1:], []) + far

    own_hi, own_lo, times = own_rows(place, counts, own_pay)
    theirs, mine = pairs(place, counts, occ_energy, own_hi, own_lo, times, virt_energy.reshape(1, V), parts)

    mine = mine + lax.ppermute(theirs, "c", [(0, 1), (1, 0)])
    pieces = lax.all_to_all(mine, "y", split_axis=0, concat_axis=0, tiled=True)
    return jnp.sum(pieces, axis=0)


def solution(mesh):
    fine = Mesh(np.asarray(mesh.devices).reshape(NY, NC, NZ, NX), ("y", "c", "z", "x"))
    wide, grp = ("z", "x"), ("y", "c")
    placed = (P(None, wide, None), P(), P(), P(), P(None, grp, None))
    return jax.shard_map(
        per_device, mesh=fine, in_specs=placed, out_specs=P(wide, grp, None), check_vma=False
    )
```

```python
import jax
import jax.numpy as jnp
import numpy as np
from jax import lax
from jax.experimental import pallas as pl
from jax.experimental.pallas import tpu as pltpu
from jax.sharding import Mesh, PartitionSpec as P

NAUX = 1024
OCC_DEV = 2
CAP = 40
V = 256
NY, NC, NZ, NX = 8, 2, 8, 4
BLK = 64
PAD = 48
MIB = 1 << 20


def split_hi_lo(x):
    hi = x.astype(jnp.bfloat16)
    lo = (x - hi.astype(jnp.float32)).astype(jnp.bfloat16)
    return hi, lo


def dot3(ah, al, bh, bl):
    def mm(a, b):
        return lax.dot_general(a, b, (((1,), (0,)), ((), ())), preferred_element_type=jnp.float32)

    return mm(ah, bh) + mm(ah, bl) + mm(al, bh)


def put_rows(dense, off, cols, block):
    base = pl.multiple_of(off // 8 * 8, 8)
    shift = off - base
    before = lax.broadcasted_iota(jnp.int32, (8, block.shape[1]), 0) < shift
    held = dense[pl.ds(base, 8), cols]
    for k in range(CAP // 8):
        turned = pltpu.roll(block[k * 8:(k + 1) * 8, :], shift, 0)
        dense[pl.ds(base + k * 8, 8), cols] = jnp.where(before, held, turned)
        held = turned
    dense[pl.ds(base + CAP, 8), cols] = held


def own_rows_kernel(place, counts, own_ref, other_ref, hi_ref, lo_ref, times_ref, dense):
    core, u, grp = place[0], place[1], place[2]
    for w in range(2):
        block = (2 * grp + w).astype(jnp.float32)
        hits = jnp.zeros((8, V), jnp.float32)
        for y in range(NY):
            for pay in (own_ref, other_ref):
                hits = hits + (pay[y, 4 * CAP:4 * CAP + 8, :] == block).astype(jnp.float32)
        times = hits[:, :128] + hits[:, 128:] + (u == 2 * grp + w).astype(jnp.float32)
        times_ref[w] = jnp.concatenate([times, times], axis=1)

    def put(s, off):
        g = lax.rem(s + u, 16)
        t = lax.rem(s // 16 + u // 16, 2)
        y = g // 2

        def copy(ref):
            for i in range(OCC_DEV):
                rows = ref[y, pl.ds(pl.multiple_of((t * OCC_DEV + i) * CAP, 8), CAP), :]
                put_rows(dense, off, slice(i * V, (i + 1) * V), rows)

        @pl.when(lax.rem(g, 2) == core)
        def _():
            copy(own_ref)

        @pl.when(lax.rem(g, 2) != core)
        def _():
            copy(other_ref)

        return off + counts[s]

    lax.fori_loop(0, 32, put, jnp.int32(0))

    def turn(n, carry):
        k, pair = n // 4, n % 4
        first = pl.multiple_of((4 * pair + lax.rem(core + 1 + k, 2)) * BLK, BLK)
        rows = jnp.concatenate(
            [dense[pl.ds(first, BLK), :], dense[pl.ds(first + 2 * BLK, BLK), :]], axis=0
        )
        hi, lo = split_hi_lo(rows.T)
        hi_ref[:, n * 128:(n + 1) * 128] = hi
        lo_ref[:, n * 128:(n + 1) * 128] = lo
        return carry

    for n in range(8):
        turn(n, 0)


def pair_kernel(place, counts, occ, own_hi_any, own_lo_any, times, virt, most_any, *refs):
    rest, refs = refs[:NZ], refs[NZ:]
    theirs_ref, mine_ref, own_hi, own_lo, rows, dense, w_hi, w_lo, x_hi, x_lo, sems = refs
    core, u, grp = place[0], place[1], place[2]
    row_copies = [
        pltpu.make_async_copy(most_any.at[z], rows.at[z, :, pl.ds(0, 3)], sems.at[z]) for z in range(NZ)
    ]
    rest_copies = [
        pltpu.make_async_copy(
            rest[n], rows.at[lax.rem(place[3] + d + NZ, NZ), :, pl.ds(3, 1)], sems.at[NZ + 2 + n]
        )
        for n, d in enumerate((0, -1, -2, -3, -4, 1, 2, 3))
    ]
    own_copies = [
        pltpu.make_async_copy(own_hi_any, own_hi, sems.at[NZ]),
        pltpu.make_async_copy(own_lo_any, own_lo, sems.at[NZ + 1]),
    ]
    for copy in rest_copies + row_copies + own_copies:
        copy.start()
    for copy in rest_copies:
        copy.wait()

    off = jnp.int32(0)
    for z in range(NZ):
        row_copies[z].wait()
        for x in range(NX):
            for j in range(4):
                put_rows(dense, off, slice(j * V, (j + 1) * V), rows[z, x, j])
            off = off + counts[z * NX + x]

    for k in range(2):
        for y in range(NY):
            src = pl.multiple_of((2 * y + lax.rem(core + 1 + k, 2)) * BLK, BLK)
            dst = slice((k * NY + y) * BLK, (k * NY + y + 1) * BLK)
            hi, lo = split_hi_lo(dense[pl.ds(src, BLK), :])
            w_hi[dst, :] = hi
            w_lo[dst, :] = lo

    virt_row = jnp.broadcast_to(virt[...], (V, V))
    virt_sum = virt_row + virt_row.T
    for copy in own_copies:
        copy.wait()
    for j in range(4):
        cols = slice(j * V, (j + 1) * V)
        coulomb = dot3(own_hi[...], own_lo[...], w_hi[:, cols], w_lo[:, cols])
        for i in range(OCC_DEV):
            c = coulomb[i * V:(i + 1) * V, :]
            scale = times[j // 2, :1, :] / ((occ[2 * u + i] + occ[4 * grp + j]) - virt_sum)
            hi, lo = split_hi_lo((2.0 * c.T - c) * scale)
            x_hi[cols, i * V:(i + 1) * V] = hi
            x_lo[cols, i * V:(i + 1) * V] = lo

    for k, out in enumerate((theirs_ref, mine_ref)):
        part = slice(k * 512, (k + 1) * 512)
        for i in range(OCC_DEV):
            cols = slice(i * V, (i + 1) * V)
            term = dot3(w_hi[part, :], w_lo[part, :], x_hi[:, cols], x_lo[:, cols])
            for q in range(NY):
                out[q, i] = term[q * BLK:(q + 1) * BLK, :]


SMEM = pl.BlockSpec(memory_space=pltpu.SMEM)
VMEM = pl.BlockSpec(memory_space=pltpu.VMEM)
HBM = pl.BlockSpec(memory_space=pl.ANY)


def own_rows(place, counts, own_pay, other_pay):
    return pl.pallas_call(
        own_rows_kernel,
        out_shape=[jax.ShapeDtypeStruct((OCC_DEV * V, NAUX), jnp.bfloat16)] * 2
        + [jax.ShapeDtypeStruct((2, 8, V), jnp.float32)],
        in_specs=[SMEM, SMEM, VMEM, VMEM],
        out_specs=[VMEM] * 3,
        scratch_shapes=[pltpu.VMEM((NAUX + PAD, OCC_DEV * V), jnp.float32)],
        compiler_params=pltpu.CompilerParams(vmem_limit_bytes=24 * MIB),
        name="own_rows",
    )(place, counts, own_pay, other_pay)


def pairs(place, counts, occ_energy, own_hi, own_lo, times, virt, most, rest):
    part = jax.ShapeDtypeStruct((NY, OCC_DEV, BLK, V), jnp.float32)
    return pl.pallas_call(
        pair_kernel,
        out_shape=[part, part],
        in_specs=[SMEM] * 3 + [HBM, HBM, VMEM, VMEM] + [HBM] * (1 + NZ),
        out_specs=[VMEM, VMEM],
        scratch_shapes=[
            pltpu.VMEM((OCC_DEV * V, NAUX), jnp.bfloat16),
            pltpu.VMEM((OCC_DEV * V, NAUX), jnp.bfloat16),
            pltpu.VMEM((NZ, NX, 4, CAP, V), jnp.float32),
            pltpu.VMEM((NAUX + PAD, 4 * V), jnp.float32),
            pltpu.VMEM((NAUX, 4 * V), jnp.bfloat16),
            pltpu.VMEM((NAUX, 4 * V), jnp.bfloat16),
            pltpu.VMEM((4 * V, OCC_DEV * V), jnp.bfloat16),
            pltpu.VMEM((4 * V, OCC_DEV * V), jnp.bfloat16),
            pltpu.SemaphoreType.DMA((2 * NZ + 2,)),
        ],
        compiler_params=pltpu.CompilerParams(vmem_limit_bytes=50 * MIB),
        name="pairs",
    )(place, counts, occ_energy, own_hi, own_lo, times, virt, most, *rest)


def per_device(three_center, counts, occ_energy, virt_energy, match_tables):
    y, c = lax.axis_index("y"), lax.axis_index("c")
    z, x = lax.axis_index("z"), lax.axis_index("x")
    grp, pos = y * NC + c, z * NX + x
    place = jnp.stack([c, pos, grp, z]).astype(jnp.int32)

    wide_part = lax.dynamic_slice_in_dim(three_center, 4 * grp, 4, 0)
    row = lax.all_gather(wide_part, "x")
    most = lax.all_gather(row[:, :3], "z")

    axes = ("y", "c", "z", "x")
    got = []
    for t in range(2):
        to = lax.rem(grp - pos + 32, 16) + 16 * lax.rem(pos // 16 + t, 2)
        piece = lax.dynamic_slice_in_dim(three_center, OCC_DEV * to, OCC_DEV, 0)
        perm = [
            (g * 32 + s, g * 32 + (g - s) % 16 + 16 * ((s // 16 + t) % 2))
            for g in range(16) for s in range(32)
        ]
        got.append(lax.ppermute(piece, axes, perm).reshape(OCC_DEV * CAP, V))
    partners = lax.dynamic_slice_in_dim(match_tables[:, 0, :], pos, 1, 1).astype(jnp.float32)
    note = jnp.broadcast_to(jnp.repeat(partners.reshape(1, 2), 128, axis=1), (8, V))
    load = jnp.concatenate(got + [note], axis=0)
    sent = jnp.broadcast_to(load[None], (NY, 4 * CAP + 8, V))
    own_pay = lax.all_to_all(sent, "y", split_axis=0, concat_axis=0, tiled=True)

    def along_z(a, d):
        return lax.ppermute(a, "z", [(k, (k + d) % NZ) for k in range(NZ)])

    up, down = [row[:, 3:]], [row[:, 3:]]
    for step in range(3):
        up.append(along_z(up[-1], 1))
        down.append(along_z(down[-1], -1))
        if step == 1:
            own_pay, up[2], down[2] = lax.optimization_barrier((own_pay, up[2], down[2]))
    up.append(along_z(up[-1], 1))
    rest = (*up, *down[1:])

    other_pay = lax.ppermute(own_pay, "c", [(0, 1), (1, 0)])

    own_hi, own_lo, times = own_rows(place, counts, own_pay, other_pay)
    theirs, mine = pairs(place, counts, occ_energy, own_hi, own_lo, times, virt_energy.reshape(1, V), most, rest)

    mine = mine + lax.ppermute(theirs, "c", [(0, 1), (1, 0)])
    pieces = lax.all_to_all(mine, "y", split_axis=0, concat_axis=0, tiled=True)
    return jnp.sum(pieces, axis=0)


def solution(mesh):
    fine = Mesh(np.asarray(mesh.devices).reshape(NY, NC, NZ, NX), ("y", "c", "z", "x"))
    wide, grp = ("z", "x"), ("y", "c")
    placed = (P(None, wide, None), P(), P(), P(), P(None, grp, None))
    return jax.shard_map(
        per_device, mesh=fine, in_specs=placed, out_specs=P(wide, grp, None), check_vma=False
    )
```

```python
import jax
import jax.numpy as jnp
import numpy as np
from jax import lax
from jax.experimental import pallas as pl
from jax.experimental.pallas import tpu as pltpu
from jax.sharding import Mesh, PartitionSpec as P

NAUX = 1024
OCC_DEV = 2
CAP = 40
V = 256
NY, NC, NZ, NX = 8, 2, 8, 4
BLK = 64
PAD = 48
MIB = 1 << 20


def split_hi_lo(x):
    hi = x.astype(jnp.bfloat16)
    lo = (x - hi.astype(jnp.float32)).astype(jnp.bfloat16)
    return hi, lo


def dot3(ah, al, bh, bl):
    def mm(a, b):
        return lax.dot_general(a, b, (((1,), (0,)), ((), ())), preferred_element_type=jnp.float32)

    return mm(ah, bh) + mm(ah, bl) + mm(al, bh)


def put_rows(dense, off, cols, block):
    base = pl.multiple_of(off // 8 * 8, 8)
    shift = off - base
    before = lax.broadcasted_iota(jnp.int32, (8, block.shape[1]), 0) < shift
    held = dense[pl.ds(base, 8), cols]
    for k in range(CAP // 8):
        turned = pltpu.roll(block[k * 8:(k + 1) * 8, :], shift, 0)
        dense[pl.ds(base + k * 8, 8), cols] = jnp.where(before, held, turned)
        held = turned
    dense[pl.ds(base + CAP, 8), cols] = held


def own_rows_kernel(place, counts, own_ref, other_ref, hi_ref, lo_ref, times_ref, dense):
    core, u, grp = place[0], place[1], place[2]
    for w in range(2):
        block = (2 * grp + w).astype(jnp.float32)
        hits = jnp.zeros((8, V), jnp.float32)
        for y in range(NY):
            for pay in (own_ref, other_ref):
                hits = hits + (pay[y, 4 * CAP:4 * CAP + 8, :] == block).astype(jnp.float32)
        times = hits[:, :128] + hits[:, 128:] + (u == 2 * grp + w).astype(jnp.float32)
        times_ref[w] = jnp.concatenate([times, times], axis=1)

    def put(s, off):
        g = lax.rem(s + u, 16)
        t = lax.rem(s // 16 + u // 16, 2)
        y = g // 2

        def copy(ref):
            for i in range(OCC_DEV):
                rows = ref[y, pl.ds(pl.multiple_of((t * OCC_DEV + i) * CAP, 8), CAP), :]
                put_rows(dense, off, slice(i * V, (i + 1) * V), rows)

        @pl.when(lax.rem(g, 2) == core)
        def _():
            copy(own_ref)

        @pl.when(lax.rem(g, 2) != core)
        def _():
            copy(other_ref)

        return off + counts[s]

    lax.fori_loop(0, 32, put, jnp.int32(0))

    def turn(n, carry):
        k, pair = n // 4, n % 4
        first = pl.multiple_of((4 * pair + lax.rem(core + 1 + k, 2)) * BLK, BLK)
        rows = jnp.concatenate(
            [dense[pl.ds(first, BLK), :], dense[pl.ds(first + 2 * BLK, BLK), :]], axis=0
        )
        hi, lo = split_hi_lo(rows.T)
        hi_ref[:, n * 128:(n + 1) * 128] = hi
        lo_ref[:, n * 128:(n + 1) * 128] = lo
        return carry

    for n in range(8):
        turn(n, 0)


def pair_kernel(place, counts, occ, own_hi_any, own_lo_any, times, virt, wide_any,
                theirs_ref, w_hi, w_lo, x_hi, x_lo, own_hi, own_lo, rows, dense, sems):
    core, u, grp = place[0], place[1], place[2]
    row_copies = [pltpu.make_async_copy(wide_any.at[z], rows.at[z], sems.at[z]) for z in range(NZ)]
    own_copies = [
        pltpu.make_async_copy(own_hi_any, own_hi, sems.at[NZ]),
        pltpu.make_async_copy(own_lo_any, own_lo, sems.at[NZ + 1]),
    ]
    for copy in row_copies + own_copies:
        copy.start()

    off = jnp.int32(0)
    for z in range(NZ):
        row_copies[z].wait()
        for x in range(NX):
            for j in range(4):
                put_rows(dense, off, slice(j * V, (j + 1) * V), rows[z, x, j])
            off = off + counts[z * NX + x]

    for k in range(2):
        for y in range(NY):
            src = pl.multiple_of((2 * y + lax.rem(core + 1 + k, 2)) * BLK, BLK)
            dst = slice((k * NY + y) * BLK, (k * NY + y + 1) * BLK)
            hi, lo = split_hi_lo(dense[pl.ds(src, BLK), :])
            w_hi[dst, :] = hi
            w_lo[dst, :] = lo

    virt_row = jnp.broadcast_to(virt[...], (V, V))
    virt_sum = virt_row + virt_row.T
    for copy in own_copies:
        copy.wait()
    for j in range(4):
        cols = slice(j * V, (j + 1) * V)
        coulomb = dot3(own_hi[...], own_lo[...], w_hi[:, cols], w_lo[:, cols])
        for i in range(OCC_DEV):
            c = coulomb[i * V:(i + 1) * V, :]
            scale = times[j // 2, :1, :] / ((occ[2 * u + i] + occ[4 * grp + j]) - virt_sum)
            hi, lo = split_hi_lo((2.0 * c.T - c) * scale)
            x_hi[cols, i * V:(i + 1) * V] = hi
            x_lo[cols, i * V:(i + 1) * V] = lo

    put_terms(theirs_ref, slice(0, 512), w_hi, w_lo, x_hi, x_lo)


def put_terms(out, part, w_hi, w_lo, x_hi, x_lo):
    for i in range(OCC_DEV):
        cols = slice(i * V, (i + 1) * V)
        term = dot3(w_hi[part, :], w_lo[part, :], x_hi[:, cols], x_lo[:, cols])
        for q in range(NY):
            out[q, i] = term[q * BLK:(q + 1) * BLK, :]


def mine_kernel(w_hi, w_lo, x_hi, x_lo, mine_ref):
    put_terms(mine_ref, slice(512, 1024), w_hi, w_lo, x_hi, x_lo)


SMEM = pl.BlockSpec(memory_space=pltpu.SMEM)
VMEM = pl.BlockSpec(memory_space=pltpu.VMEM)
HBM = pl.BlockSpec(memory_space=pl.ANY)


def own_rows(place, counts, own_pay, other_pay):
    return pl.pallas_call(
        own_rows_kernel,
        out_shape=[jax.ShapeDtypeStruct((OCC_DEV * V, NAUX), jnp.bfloat16)] * 2
        + [jax.ShapeDtypeStruct((2, 8, V), jnp.float32)],
        in_specs=[SMEM, SMEM, VMEM, VMEM],
        out_specs=[VMEM] * 3,
        scratch_shapes=[pltpu.VMEM((NAUX + PAD, OCC_DEV * V), jnp.float32)],
        compiler_params=pltpu.CompilerParams(vmem_limit_bytes=24 * MIB),
        name="own_rows",
    )(place, counts, own_pay, other_pay)


def pairs(place, counts, occ_energy, own_hi, own_lo, times, virt, wide_all):
    part = jax.ShapeDtypeStruct((NY, OCC_DEV, BLK, V), jnp.float32)
    wide_split = jax.ShapeDtypeStruct((NAUX, 4 * V), jnp.bfloat16)
    weights = jax.ShapeDtypeStruct((4 * V, OCC_DEV * V), jnp.bfloat16)
    return pl.pallas_call(
        pair_kernel,
        out_shape=[part] + [wide_split] * 2 + [weights] * 2,
        in_specs=[SMEM] * 3 + [HBM, HBM, VMEM, VMEM, HBM],
        out_specs=[VMEM] * 5,
        scratch_shapes=[
            pltpu.VMEM((OCC_DEV * V, NAUX), jnp.bfloat16),
            pltpu.VMEM((OCC_DEV * V, NAUX), jnp.bfloat16),
            pltpu.VMEM((NZ, NX, 4, CAP, V), jnp.float32),
            pltpu.VMEM((NAUX + PAD, 4 * V), jnp.float32),
            pltpu.SemaphoreType.DMA((NZ + 2,)),
        ],
        compiler_params=pltpu.CompilerParams(vmem_limit_bytes=40 * MIB),
        name="pairs",
    )(place, counts, occ_energy, own_hi, own_lo, times, virt, wide_all)


def own_core_rows(*operands):
    return pl.pallas_call(
        mine_kernel,
        out_shape=jax.ShapeDtypeStruct((NY, OCC_DEV, BLK, V), jnp.float32),
        in_specs=[VMEM] * 4,
        out_specs=VMEM,
        compiler_params=pltpu.CompilerParams(vmem_limit_bytes=32 * MIB),
        cost_estimate=pl.CostEstimate(flops=6 * 512 * 512 * 1024, bytes_accessed=8 * MIB, transcendentals=0),
        name="own_core_rows",
    )(*operands)


def per_device(three_center, counts, occ_energy, virt_energy, match_tables):
    y, c = lax.axis_index("y"), lax.axis_index("c")
    z, x = lax.axis_index("z"), lax.axis_index("x")
    grp, pos = y * NC + c, z * NX + x
    place = jnp.stack([c, pos, grp]).astype(jnp.int32)

    wide_part = lax.dynamic_slice_in_dim(three_center, 4 * grp, 4, 0)
    wide_all = lax.all_gather(lax.all_gather(wide_part, "x"), "z")

    axes = ("y", "c", "z", "x")
    got = []
    for t in range(2):
        to = lax.rem(grp - pos + 32, 16) + 16 * lax.rem(pos // 16 + t, 2)
        piece = lax.dynamic_slice_in_dim(three_center, OCC_DEV * to, OCC_DEV, 0)
        perm = [
            (g * 32 + s, g * 32 + (g - s) % 16 + 16 * ((s // 16 + t) % 2))
            for g in range(16) for s in range(32)
        ]
        got.append(lax.ppermute(piece, axes, perm).reshape(OCC_DEV * CAP, V))
    partners = lax.dynamic_slice_in_dim(match_tables[:, 0, :], pos, 1, 1).astype(jnp.float32)
    note = jnp.broadcast_to(jnp.repeat(partners.reshape(1, 2), 128, axis=1), (8, V))
    load = jnp.concatenate(got + [note], axis=0)
    sent = jnp.broadcast_to(load[None], (NY, 4 * CAP + 8, V))
    own_pay = lax.all_to_all(sent, "y", split_axis=0, concat_axis=0, tiled=True)
    other_pay = lax.ppermute(own_pay, "c", [(0, 1), (1, 0)])

    own_hi, own_lo, times = own_rows(place, counts, own_pay, other_pay)
    theirs, *split = pairs(place, counts, occ_energy, own_hi, own_lo, times, virt_energy.reshape(1, V), wide_all)

    sums = lax.ppermute(theirs, "c", [(0, 1), (1, 0)])
    mine = own_core_rows(*split) + sums
    pieces = lax.all_to_all(mine, "y", split_axis=0, concat_axis=0, tiled=True)
    return jnp.sum(pieces, axis=0)


def solution(mesh):
    fine = Mesh(np.asarray(mesh.devices).reshape(NY, NC, NZ, NX), ("y", "c", "z", "x"))
    wide, grp = ("z", "x"), ("y", "c")
    placed = (P(None, wide, None), P(), P(), P(), P(None, grp, None))
    return jax.shard_map(
        per_device, mesh=fine, in_specs=placed, out_specs=P(wide, grp, None), check_vma=False
    )
```

```python
import jax
import jax.numpy as jnp
import numpy as np
from jax import lax
from jax.experimental import pallas as pl
from jax.experimental.pallas import tpu as pltpu
from jax.sharding import Mesh, PartitionSpec as P

NAUX = 1024
OCC_DEV = 2
CAP = 40
V = 256
NY, NC, NZ, NX = 8, 2, 8, 4
BLK = 64
PAD = 48
MIB = 1 << 20


def split_hi_lo(x):
    hi = x.astype(jnp.bfloat16)
    lo = (x - hi.astype(jnp.float32)).astype(jnp.bfloat16)
    return hi, lo


def dot3(ah, al, bh, bl):
    def mm(a, b):
        return lax.dot_general(a, b, (((1,), (0,)), ((), ())), preferred_element_type=jnp.float32)

    return mm(ah, bh) + mm(ah, bl) + mm(al, bh)


def put_rows(dense, off, cols, block):
    base = pl.multiple_of(off // 8 * 8, 8)
    shift = off - base
    before = lax.broadcasted_iota(jnp.int32, (8, block.shape[1]), 0) < shift
    held = dense[pl.ds(base, 8), cols]
    for k in range(CAP // 8):
        turned = pltpu.roll(block[k * 8:(k + 1) * 8, :], shift, 0)
        dense[pl.ds(base + k * 8, 8), cols] = jnp.where(before, held, turned)
        held = turned
    dense[pl.ds(base + CAP, 8), cols] = held


def own_rows_kernel(place, counts, own_ref, other_ref, hi_ref, lo_ref, times_ref, dense):
    core, u, grp = place[0], place[1], place[2]
    for w in range(2):
        block = (2 * grp + w).astype(jnp.float32)
        hits = jnp.zeros((8, V), jnp.float32)
        for y in range(NY):
            for pay in (own_ref, other_ref):
                hits = hits + (pay[y, 4 * CAP:4 * CAP + 8, :] == block).astype(jnp.float32)
        times = hits[:, :128] + hits[:, 128:] + (u == 2 * grp + w).astype(jnp.float32)
        times_ref[w] = jnp.concatenate([times, times], axis=1)

    def put(s, off):
        g = lax.rem(s + u, 16)
        t = lax.rem(s // 16 + u // 16, 2)
        y = g // 2

        def copy(ref):
            for i in range(OCC_DEV):
                rows = ref[y, pl.ds(pl.multiple_of((t * OCC_DEV + i) * CAP, 8), CAP), :]
                put_rows(dense, off, slice(i * V, (i + 1) * V), rows)

        @pl.when(lax.rem(g, 2) == core)
        def _():
            copy(own_ref)

        @pl.when(lax.rem(g, 2) != core)
        def _():
            copy(other_ref)

        return off + counts[s]

    lax.fori_loop(0, 32, put, jnp.int32(0))

    def turn(n, carry):
        k, pair = n // 4, n % 4
        first = pl.multiple_of((4 * pair + lax.rem(core + 1 + k, 2)) * BLK, BLK)
        rows = jnp.concatenate(
            [dense[pl.ds(first, BLK), :], dense[pl.ds(first + 2 * BLK, BLK), :]], axis=0
        )
        hi, lo = split_hi_lo(rows.T)
        hi_ref[:, n * 128:(n + 1) * 128] = hi
        lo_ref[:, n * 128:(n + 1) * 128] = lo
        return carry

    for n in range(8):
        turn(n, 0)


def pair_kernel(place, counts, occ, own_hi, own_lo, times, virt, wide_any,
                theirs_ref, w_hi, w_lo, x_hi, x_lo, rows, dense, sems):
    core, u, grp = place[0], place[1], place[2]
    row_copies = [pltpu.make_async_copy(wide_any.at[z], rows.at[z], sems.at[z]) for z in range(NZ)]
    for copy in row_copies:
        copy.start()

    off = jnp.int32(0)
    for z in range(NZ):
        row_copies[z].wait()
        for x in range(NX):
            for j in range(4):
                put_rows(dense, off, slice(j * V, (j + 1) * V), rows[z, x, j])
            off = off + counts[z * NX + x]

    for k in range(2):
        for y in range(NY):
            src = pl.multiple_of((2 * y + lax.rem(core + 1 + k, 2)) * BLK, BLK)
            dst = slice((k * NY + y) * BLK, (k * NY + y + 1) * BLK)
            hi, lo = split_hi_lo(dense[pl.ds(src, BLK), :])
            w_hi[dst, :] = hi
            w_lo[dst, :] = lo

    virt_row = jnp.broadcast_to(virt[...], (V, V))
    virt_sum = virt_row + virt_row.T
    for j in range(4):
        cols = slice(j * V, (j + 1) * V)
        coulomb = dot3(own_hi[...], own_lo[...], w_hi[:, cols], w_lo[:, cols])
        for i in range(OCC_DEV):
            c = coulomb[i * V:(i + 1) * V, :]
            scale = times[j // 2, :1, :] / ((occ[2 * u + i] + occ[4 * grp + j]) - virt_sum)
            hi, lo = split_hi_lo((2.0 * c.T - c) * scale)
            x_hi[cols, i * V:(i + 1) * V] = hi
            x_lo[cols, i * V:(i + 1) * V] = lo

    put_terms(theirs_ref, slice(0, 512), w_hi, w_lo, x_hi, x_lo)


def put_terms(out, part, w_hi, w_lo, x_hi, x_lo):
    for i in range(OCC_DEV):
        cols = slice(i * V, (i + 1) * V)
        term = dot3(w_hi[part, :], w_lo[part, :], x_hi[:, cols], x_lo[:, cols])
        for q in range(NY):
            out[q, i] = term[q * BLK:(q + 1) * BLK, :]


def mine_kernel(w_hi, w_lo, x_hi, x_lo, mine_ref):
    put_terms(mine_ref, slice(512, 1024), w_hi, w_lo, x_hi, x_lo)


SMEM = pl.BlockSpec(memory_space=pltpu.SMEM)
VMEM = pl.BlockSpec(memory_space=pltpu.VMEM)
HBM = pl.BlockSpec(memory_space=pl.ANY)


def own_rows(place, counts, own_pay, other_pay):
    return pl.pallas_call(
        own_rows_kernel,
        out_shape=[jax.ShapeDtypeStruct((OCC_DEV * V, NAUX), jnp.bfloat16)] * 2
        + [jax.ShapeDtypeStruct((2, 8, V), jnp.float32)],
        in_specs=[SMEM, SMEM, VMEM, VMEM],
        out_specs=[VMEM] * 3,
        scratch_shapes=[pltpu.VMEM((NAUX + PAD, OCC_DEV * V), jnp.float32)],
        compiler_params=pltpu.CompilerParams(vmem_limit_bytes=24 * MIB),
        name="own_rows",
    )(place, counts, own_pay, other_pay)


def pairs(place, counts, occ_energy, own_hi, own_lo, times, virt, wide_all):
    part = jax.ShapeDtypeStruct((NY, OCC_DEV, BLK, V), jnp.float32)
    wide_split = jax.ShapeDtypeStruct((NAUX, 4 * V), jnp.bfloat16)
    weights = jax.ShapeDtypeStruct((4 * V, OCC_DEV * V), jnp.bfloat16)
    return pl.pallas_call(
        pair_kernel,
        out_shape=[part] + [wide_split] * 2 + [weights] * 2,
        in_specs=[SMEM] * 3 + [VMEM] * 4 + [HBM],
        out_specs=[VMEM] * 5,
        scratch_shapes=[
            pltpu.VMEM((NZ, NX, 4, CAP, V), jnp.float32),
            pltpu.VMEM((NAUX + PAD, 4 * V), jnp.float32),
            pltpu.SemaphoreType.DMA((NZ,)),
        ],
        compiler_params=pltpu.CompilerParams(vmem_limit_bytes=40 * MIB),
        name="pairs",
    )(place, counts, occ_energy, own_hi, own_lo, times, virt, wide_all)


def own_core_rows(*operands):
    return pl.pallas_call(
        mine_kernel,
        out_shape=jax.ShapeDtypeStruct((NY, OCC_DEV, BLK, V), jnp.float32),
        in_specs=[VMEM] * 4,
        out_specs=VMEM,
        compiler_params=pltpu.CompilerParams(vmem_limit_bytes=32 * MIB),
        cost_estimate=pl.CostEstimate(flops=6 * 512 * 512 * 1024, bytes_accessed=8 * MIB, transcendentals=0),
        name="own_core_rows",
    )(*operands)


def per_device(three_center, counts, occ_energy, virt_energy, match_tables):
    y, c = lax.axis_index("y"), lax.axis_index("c")
    z, x = lax.axis_index("z"), lax.axis_index("x")
    grp, pos = y * NC + c, z * NX + x
    place = jnp.stack([c, pos, grp]).astype(jnp.int32)

    wide_part = lax.dynamic_slice_in_dim(three_center, 4 * grp, 4, 0)
    wide_all = lax.all_gather(lax.all_gather(wide_part, "x"), "z")

    axes = ("y", "c", "z", "x")
    got = []
    for t in range(2):
        to = lax.rem(grp - pos + 32, 16) + 16 * lax.rem(pos // 16 + t, 2)
        piece = lax.dynamic_slice_in_dim(three_center, OCC_DEV * to, OCC_DEV, 0)
        perm = [
            (g * 32 + s, g * 32 + (g - s) % 16 + 16 * ((s // 16 + t) % 2))
            for g in range(16) for s in range(32)
        ]
        got.append(lax.ppermute(piece, axes, perm).reshape(OCC_DEV * CAP, V))
    partners = lax.dynamic_slice_in_dim(match_tables[:, 0, :], pos, 1, 1).astype(jnp.float32)
    note = jnp.broadcast_to(jnp.repeat(partners.reshape(1, 2), 128, axis=1), (8, V))
    load = jnp.concatenate(got + [note], axis=0)
    sent = jnp.broadcast_to(load[None], (NY, 4 * CAP + 8, V))
    own_pay = lax.all_to_all(sent, "y", split_axis=0, concat_axis=0, tiled=True)
    other_pay = lax.ppermute(own_pay, "c", [(0, 1), (1, 0)])

    own_hi, own_lo, times = own_rows(place, counts, own_pay, other_pay)
    theirs, *split = pairs(place, counts, occ_energy, own_hi, own_lo, times, virt_energy.reshape(1, V), wide_all)

    sums = lax.ppermute(theirs, "c", [(0, 1), (1, 0)])
    mine = own_core_rows(*split) + sums
    pieces = lax.all_to_all(mine, "y", split_axis=0, concat_axis=0, tiled=True)
    return jnp.sum(pieces, axis=0)


def solution(mesh):
    fine = Mesh(np.asarray(mesh.devices).reshape(NY, NC, NZ, NX), ("y", "c", "z", "x"))
    wide, grp = ("z", "x"), ("y", "c")
    placed = (P(None, wide, None), P(), P(), P(), P(None, grp, None))
    return jax.shard_map(
        per_device, mesh=fine, in_specs=placed, out_specs=P(wide, grp, None), check_vma=False
    )
```

```python
import jax
import jax.numpy as jnp
import numpy as np
from jax import lax
from jax.experimental import pallas as pl
from jax.experimental.pallas import tpu as pltpu
from jax.sharding import Mesh, PartitionSpec as P

NAUX = 1024
OCC_DEV = 2
CAP = 40
V = 256
NY, NC, NZ, NX = 8, 2, 8, 4
BLK = 64
PAD = 48
MIB = 1 << 20


def split_hi_lo(x):
    hi = x.astype(jnp.bfloat16)
    lo = (x - hi.astype(jnp.float32)).astype(jnp.bfloat16)
    return hi, lo


def dot3(ah, al, bh, bl):
    def mm(a, b):
        return lax.dot_general(a, b, (((1,), (0,)), ((), ())), preferred_element_type=jnp.float32)

    return mm(ah, bh) + mm(ah, bl) + mm(al, bh)


def put_rows(dense, off, cols, block):
    base = pl.multiple_of(off // 8 * 8, 8)
    shift = off - base
    before = lax.broadcasted_iota(jnp.int32, (8, block.shape[1]), 0) < shift
    held = dense[pl.ds(base, 8), cols]
    for k in range(CAP // 8):
        turned = pltpu.roll(block[k * 8:(k + 1) * 8, :], shift, 0)
        dense[pl.ds(base + k * 8, 8), cols] = jnp.where(before, held, turned)
        held = turned
    dense[pl.ds(base + CAP, 8), cols] = held


def own_rows_kernel(place, counts, own_ref, other_ref, hi_ref, lo_ref, times_ref, dense):
    core, u, grp = place[0], place[1], place[2]
    for w in range(2):
        block = (2 * grp + w).astype(jnp.float32)
        hits = jnp.zeros((8, V), jnp.float32)
        for y in range(NY):
            for pay in (own_ref, other_ref):
                hits = hits + (pay[y, 4 * CAP:4 * CAP + 8, :] == block).astype(jnp.float32)
        times = hits[:, :128] + hits[:, 128:] + (u == 2 * grp + w).astype(jnp.float32)
        times_ref[w] = jnp.concatenate([times, times], axis=1)

    def put(s, off):
        g = lax.rem(s + u, 16)
        t = lax.rem(s // 16 + u // 16, 2)
        y = g // 2

        def copy(ref):
            for i in range(OCC_DEV):
                rows = ref[y, pl.ds(pl.multiple_of((t * OCC_DEV + i) * CAP, 8), CAP), :]
                put_rows(dense, off, slice(i * V, (i + 1) * V), rows)

        @pl.when(lax.rem(g, 2) == core)
        def _():
            copy(own_ref)

        @pl.when(lax.rem(g, 2) != core)
        def _():
            copy(other_ref)

        return off + counts[s]

    lax.fori_loop(0, 32, put, jnp.int32(0))

    def turn(n, carry):
        k, pair = n // 4, n % 4
        first = pl.multiple_of((4 * pair + lax.rem(core + 1 + k, 2)) * BLK, BLK)
        rows = jnp.concatenate(
            [dense[pl.ds(first, BLK), :], dense[pl.ds(first + 2 * BLK, BLK), :]], axis=0
        )
        hi, lo = split_hi_lo(rows.T)
        hi_ref[:, n * 128:(n + 1) * 128] = hi
        lo_ref[:, n * 128:(n + 1) * 128] = lo
        return carry

    for n in range(8):
        turn(n, 0)


def pair_kernel(place, counts, occ, own_hi, own_lo, times, virt, wide_any,
                theirs_ref, w_hi, w_lo, x_hi, x_lo, rows, dense, sems):
    core, u, grp = place[0], place[1], place[2]
    row_copies = [
        pltpu.make_async_copy(wide_any.at[n // 2, pl.ds(n % 2 * 2, 2)], rows.at[n // 2, pl.ds(n % 2 * 2, 2)], sems.at[n])
        for n in range(2 * NZ)
    ]
    for copy in row_copies:
        copy.start()

    off = jnp.int32(0)
    for z in range(NZ):
        for x in range(NX):
            if x % 2 == 0:
                row_copies[2 * z + x // 2].wait()
            for j in range(4):
                put_rows(dense, off, slice(j * V, (j + 1) * V), rows[z, x, j])
            off = off + counts[z * NX + x]

    for k in range(2):
        for y in range(NY):
            src = pl.multiple_of((2 * y + lax.rem(core + 1 + k, 2)) * BLK, BLK)
            dst = slice((k * NY + y) * BLK, (k * NY + y + 1) * BLK)
            hi, lo = split_hi_lo(dense[pl.ds(src, BLK), :])
            w_hi[dst, :] = hi
            w_lo[dst, :] = lo

    virt_row = jnp.broadcast_to(virt[...], (V, V))
    virt_sum = virt_row + virt_row.T
    for j in range(4):
        cols = slice(j * V, (j + 1) * V)
        coulomb = dot3(own_hi[...], own_lo[...], w_hi[:, cols], w_lo[:, cols])
        for i in range(OCC_DEV):
            c = coulomb[i * V:(i + 1) * V, :]
            scale = times[j // 2, :1, :] / ((occ[2 * u + i] + occ[4 * grp + j]) - virt_sum)
            hi, lo = split_hi_lo((2.0 * c.T - c) * scale)
            x_hi[cols, i * V:(i + 1) * V] = hi
            x_lo[cols, i * V:(i + 1) * V] = lo

    put_terms(theirs_ref, slice(0, 512), w_hi, w_lo, x_hi, x_lo)


def put_terms(out, part, w_hi, w_lo, x_hi, x_lo):
    for i in range(OCC_DEV):
        cols = slice(i * V, (i + 1) * V)
        term = dot3(w_hi[part, :], w_lo[part, :], x_hi[:, cols], x_lo[:, cols])
        for q in range(NY):
            out[q, i] = term[q * BLK:(q + 1) * BLK, :]


def mine_kernel(w_hi, w_lo, x_hi, x_lo, mine_ref):
    put_terms(mine_ref, slice(512, 1024), w_hi, w_lo, x_hi, x_lo)


SMEM = pl.BlockSpec(memory_space=pltpu.SMEM)
VMEM = pl.BlockSpec(memory_space=pltpu.VMEM)
HBM = pl.BlockSpec(memory_space=pl.ANY)


def own_rows(place, counts, own_pay, other_pay):
    return pl.pallas_call(
        own_rows_kernel,
        out_shape=[jax.ShapeDtypeStruct((OCC_DEV * V, NAUX), jnp.bfloat16)] * 2
        + [jax.ShapeDtypeStruct((2, 8, V), jnp.float32)],
        in_specs=[SMEM, SMEM, VMEM, VMEM],
        out_specs=[VMEM] * 3,
        scratch_shapes=[pltpu.VMEM((NAUX + PAD, OCC_DEV * V), jnp.float32)],
        compiler_params=pltpu.CompilerParams(vmem_limit_bytes=24 * MIB),
        name="own_rows",
    )(place, counts, own_pay, other_pay)


def pairs(place, counts, occ_energy, own_hi, own_lo, times, virt, wide_all):
    part = jax.ShapeDtypeStruct((NY, OCC_DEV, BLK, V), jnp.float32)
    wide_split = jax.ShapeDtypeStruct((NAUX, 4 * V), jnp.bfloat16)
    weights = jax.ShapeDtypeStruct((4 * V, OCC_DEV * V), jnp.bfloat16)
    return pl.pallas_call(
        pair_kernel,
        out_shape=[part] + [wide_split] * 2 + [weights] * 2,
        in_specs=[SMEM] * 3 + [VMEM] * 4 + [HBM],
        out_specs=[VMEM] * 5,
        scratch_shapes=[
            pltpu.VMEM((NZ, NX, 4, CAP, V), jnp.float32),
            pltpu.VMEM((NAUX + PAD, 4 * V), jnp.float32),
            pltpu.SemaphoreType.DMA((2 * NZ,)),
        ],
        compiler_params=pltpu.CompilerParams(vmem_limit_bytes=40 * MIB),
        name="pairs",
    )(place, counts, occ_energy, own_hi, own_lo, times, virt, wide_all)


def own_core_rows(*operands):
    return pl.pallas_call(
        mine_kernel,
        out_shape=jax.ShapeDtypeStruct((NY, OCC_DEV, BLK, V), jnp.float32),
        in_specs=[VMEM] * 4,
        out_specs=VMEM,
        compiler_params=pltpu.CompilerParams(vmem_limit_bytes=32 * MIB),
        cost_estimate=pl.CostEstimate(flops=6 * 512 * 512 * 1024, bytes_accessed=8 * MIB, transcendentals=0),
        name="own_core_rows",
    )(*operands)


def per_device(three_center, counts, occ_energy, virt_energy, match_tables):
    y, c = lax.axis_index("y"), lax.axis_index("c")
    z, x = lax.axis_index("z"), lax.axis_index("x")
    grp, pos = y * NC + c, z * NX + x
    place = jnp.stack([c, pos, grp]).astype(jnp.int32)

    wide_part = lax.dynamic_slice_in_dim(three_center, 4 * grp, 4, 0)
    wide_all = lax.all_gather(lax.all_gather(wide_part, "x"), "z")

    axes = ("y", "c", "z", "x")
    got = []
    for t in range(2):
        to = lax.rem(grp - pos + 32, 16) + 16 * lax.rem(pos // 16 + t, 2)
        piece = lax.dynamic_slice_in_dim(three_center, OCC_DEV * to, OCC_DEV, 0)
        perm = [
            (g * 32 + s, g * 32 + (g - s) % 16 + 16 * ((s // 16 + t) % 2))
            for g in range(16) for s in range(32)
        ]
        got.append(lax.ppermute(piece, axes, perm).reshape(OCC_DEV * CAP, V))
    partners = lax.dynamic_slice_in_dim(match_tables[:, 0, :], pos, 1, 1).astype(jnp.float32)
    note = jnp.broadcast_to(jnp.repeat(partners.reshape(1, 2), 128, axis=1), (8, V))
    load = jnp.concatenate(got + [note], axis=0)
    sent = jnp.broadcast_to(load[None], (NY, 4 * CAP + 8, V))
    own_pay = lax.all_to_all(sent, "y", split_axis=0, concat_axis=0, tiled=True)
    other_pay = lax.ppermute(own_pay, "c", [(0, 1), (1, 0)])

    own_hi, own_lo, times = own_rows(place, counts, own_pay, other_pay)
    theirs, *split = pairs(place, counts, occ_energy, own_hi, own_lo, times, virt_energy.reshape(1, V), wide_all)

    sums = lax.ppermute(theirs, "c", [(0, 1), (1, 0)])
    mine = own_core_rows(*split) + sums
    pieces = lax.all_to_all(mine, "y", split_axis=0, concat_axis=0, tiled=True)
    return jnp.sum(pieces, axis=0)


def solution(mesh):
    fine = Mesh(np.asarray(mesh.devices).reshape(NY, NC, NZ, NX), ("y", "c", "z", "x"))
    wide, grp = ("z", "x"), ("y", "c")
    placed = (P(None, wide, None), P(), P(), P(), P(None, grp, None))
    return jax.shard_map(
        per_device, mesh=fine, in_specs=placed, out_specs=P(wide, grp, None), check_vma=False
    )
```
